32 devices in a mesh: ctx: 4 (over y, x), exp: 8 (over z, core).
Axes of the slice: x: 2, y: 2, z: 4, core: 2. Of those that a mesh axis runs over, the one named last changes fastest.
Arguments:
- queries: bfloat16 [8, 512, 4096], P('exp', 'ctx'), may hold values from -6 to 6
- keys: bfloat16 [8, 512, 512], P('exp', 'ctx'), may hold values from -6 to 6
- values: bfloat16 [8, 512, 512], P('exp', 'ctx'), may hold values from -8 to 8
- resid: bfloat16 [8, 512, 2048], P('exp', 'ctx'), may hold values from -40 to 40
- out_weight: bfloat16 [4096, 2048], P('ctx', 'exp'), may hold values from -0.5 to 0.5
- norm_gain: float32 [2048], replicated, may hold values from 0.5 to 2
- expert_gate: bfloat16 [16, 2048, 768], P('exp'), may hold values from -0.125 to 0.125
- expert_up: bfloat16 [16, 2048, 768], P('exp'), may hold values from -0.125 to 0.125
- expert_down: bfloat16 [16, 768, 2048], P('exp'), may hold values from -0.4375 to 0.4375
- route_ids: int32 [8, 512, 8], P('exp', 'ctx'), may hold values from 0 to 15, as said below
- route_gates: float32 [8, 512, 8], P('exp', 'ctx'), may hold values from 0.1 to 1
Outputs:
- attn_resid: bfloat16 [8, 512, 2048], P('exp', 'ctx')
- layer_out: bfloat16 [8, 512, 2048], P('exp', 'ctx')
The draws below stay inside these ranges and needn't reach their ends.
Inputs may be any that keep to these rules, and one draw needn't show every extreme that they name: `route_ids`: each row names 8 different experts. In every block of 128 consecutive positions of a sequence (the tokens of one device) each expert is named by at most 64 rows, and one expert, the same in all blocks of a draw, by exactly 64 rows.
All inputs are finite; a program needn't handle non-finite values.
Results may differ from the reference program's by a relative error of at most 0.017.
Values may be sent and summed in bfloat16 or wider, within the bound.
No kernel may reach another device: no remote copies, remote signals or barrier semaphores. Data moves between devices by JAX's collectives and lax.ppermute only.
A program may use at most 128 MiB of HBM per device.

```python
import math
import jax
import jax.numpy as jnp
from jax import lax

D = 2048
QUERY_HEAD_COUNT = 32
KEY_VALUE_HEADS = 4
HEAD_SIZE = 128
FF = 768
TOPK = 8
TOK_DEV = 128
SEQUENCE_LENGTH = 512
SEQUENCE_COUNT = 8
EXPERTS = 16
CAP = 64


def draw_queries(key, part):
    start_offset = jnp.clip(jax.random.normal(jax.random.fold_in(key, 11), (SEQUENCE_COUNT, SEQUENCE_LENGTH, QUERY_HEAD_COUNT * HEAD_SIZE), jnp.float32), -4.0, 4.0)
    return start_offset.astype(jnp.bfloat16)


def draw_keys(key, part):
    start_offset = jnp.clip(jax.random.normal(jax.random.fold_in(key, 12), (SEQUENCE_COUNT, SEQUENCE_LENGTH, KEY_VALUE_HEADS * HEAD_SIZE), jnp.float32), -4.0, 4.0)
    return start_offset.astype(jnp.bfloat16)


def draw_resid(key, part):
    start_offset = jnp.clip(jax.random.normal(jax.random.fold_in(key, 41), (SEQUENCE_COUNT, SEQUENCE_LENGTH, D), jnp.float32), -4.0, 4.0)
    low = jnp.log(0.3)
    high = jnp.log(3.0)
    row_scale = jnp.exp(jax.random.uniform(jax.random.fold_in(key, 42), (SEQUENCE_COUNT, SEQUENCE_LENGTH, 1), jnp.float32, low, high))
    column_scale = jnp.exp(jax.random.uniform(jax.random.fold_in(key, 43), (1, 1, D), jnp.float32, low, high))
    return jnp.clip(start_offset * row_scale * column_scale, -40.0, 40.0).astype(jnp.bfloat16)


def draw_route_ids(key, part):
    block_total = SEQUENCE_COUNT * (SEQUENCE_LENGTH // TOK_DEV)
    hot_expert = jax.random.randint(jax.random.fold_in(key, 31), (), 0, EXPERTS)
    block_keys = jax.random.split(jax.random.fold_in(key, 32), block_total)

    def one_block(block_key):
        cycle = jax.random.permutation(jax.random.fold_in(block_key, 1), EXPERTS - 1).astype(jnp.int32)
        token_order = jax.random.permutation(jax.random.fold_in(block_key, 2), TOK_DEV).astype(jnp.int32)
        turn = jax.random.randint(jax.random.fold_in(block_key, 3), (TOK_DEV, 1), 0, TOPK)
        place = jnp.arange(TOK_DEV, dtype=jnp.int32)[:, None]
        column = jnp.arange(TOPK, dtype=jnp.int32)[None, :]
        is_hot = place < CAP
        index_hot = place * (TOPK - 1) + column - 1
        index_rest = CAP * (TOPK - 1) + (place - CAP) * TOPK + column
        entry = jnp.where(is_hot, index_hot, index_rest)
        others = cycle[jnp.mod(entry, EXPERTS - 1)]
        others = others + (others >= hot_expert).astype(jnp.int32)
        picked = jnp.where(is_hot & (column == 0), hot_expert, others)
        rotated = jnp.take_along_axis(picked, jnp.mod(column + turn, TOPK), axis=1)
        return jnp.zeros((TOK_DEV, TOPK), jnp.int32).at[token_order].set(rotated)
    return jax.vmap(one_block)(block_keys).reshape(SEQUENCE_COUNT, SEQUENCE_LENGTH, TOPK)


def block_scale(stream_key, extent, pieces, low, high):
    def one(dim, blocks):
        heights = jax.random.uniform(jax.random.fold_in(jax.random.fold_in(stream_key, 6), dim), (blocks,), jnp.float32, low / len(pieces), high / len(pieces))
        return jnp.repeat(jnp.exp(heights), extent[dim] // blocks).reshape((-1,) + (1,) * (len(extent) - dim - 1))

    factor_of = one(*pieces[0])
    for cut in pieces[1:]:
        factor_of = factor_of * one(*cut)
    return factor_of


def gaussian(own_key, dims, deviation, limit, cuts=(), held_as=jnp.bfloat16):
    loudness = block_scale(own_key, dims, cuts, -0.22, 0.18) if cuts else 1.0
    values = jax.random.normal(own_key, dims, jnp.float32) * deviation * loudness
    return jnp.minimum(jnp.maximum(values, -limit), limit).astype(held_as)


def setup_inputs(seed: int = 0) -> dict:
    key_of = jax.random.split(jax.random.key(seed), 12)
    queries = draw_queries(jax.random.fold_in(key_of[11], 71), 0)
    keys = draw_keys(jax.random.fold_in(key_of[11], 71), 0)
    values = gaussian(key_of[2], (SEQUENCE_COUNT, SEQUENCE_LENGTH, KEY_VALUE_HEADS * HEAD_SIZE), 2.0, 8.0, ((0, 8), (1, 4)))
    resid = draw_resid(jax.random.fold_in(key_of[11], 71), 0)
    out_weight = gaussian(key_of[4], (QUERY_HEAD_COUNT * HEAD_SIZE, D), HEAD_SIZE ** -0.5, 0.5, ((0, 4), (1, 8)))
    norm_gain = jnp.clip(jnp.exp(jax.random.uniform(key_of[5], (D,), jnp.float32, math.log(0.5), math.log(2.0))), 0.5, 2.0)
    expert_gate = gaussian(key_of[6], (EXPERTS, D, FF), D ** -0.5, 0.125, ((0, 8),))
    expert_up = gaussian(key_of[7], (EXPERTS, D, FF), D ** -0.5, 0.125, ((0, 8),))
    expert_down = gaussian(key_of[8], (EXPERTS, FF, D), (FF // 4) ** -0.5, 0.4375, ((0, 8),))
    route_ids = draw_route_ids(jax.random.fold_in(key_of[11], 71), 0)
    route_gates = jnp.clip(0.1 + 0.9 * jax.random.uniform(key_of[10], (SEQUENCE_COUNT, SEQUENCE_LENGTH, TOPK), jnp.float32) ** block_scale(key_of[10], (SEQUENCE_COUNT, SEQUENCE_LENGTH, TOPK), ((0, 8), (1, 4)), -0.2, 0.2), 0.1, 1.0)
    return {"queries": queries, "keys": keys, "values": values, "resid": resid, "out_weight": out_weight, "norm_gain": norm_gain, "expert_gate": expert_gate, "expert_up": expert_up, "expert_down": expert_down, "route_ids": route_ids, "route_gates": route_gates}


norm_eps = 1e-06
tile_height = 256

def attend_sequence(inputs):
    query_sequence, key_sequence, value_sequence = inputs
    sequence_length = query_sequence.shape[0]
    query_group = QUERY_HEAD_COUNT // KEY_VALUE_HEADS
    query_head_rows = query_sequence.reshape(sequence_length, KEY_VALUE_HEADS, query_group, HEAD_SIZE).astype(jnp.float32)
    key_head_rows = key_sequence.reshape(sequence_length, KEY_VALUE_HEADS, HEAD_SIZE).astype(jnp.float32)
    value_head_rows = value_sequence.reshape(sequence_length, KEY_VALUE_HEADS, HEAD_SIZE).astype(jnp.float32)
    raw_scores = jnp.einsum('tngd,und->ngtu', query_head_rows, key_head_rows) * HEAD_SIZE ** (-0.5)
    position = jnp.arange(sequence_length, dtype=jnp.int32)
    allowed = position[:, None] >= position[None, :]
    masked = jnp.where(allowed, raw_scores, -jnp.inf)
    row_top = lax.optimization_barrier(jnp.max(masked, axis=-1, keepdims=True))
    exp_scores = jnp.where(allowed, jnp.exp(masked - row_top), 0.0)
    row_total = lax.optimization_barrier(jnp.sum(exp_scores, axis=-1))
    weights = exp_scores.astype(jnp.bfloat16).astype(jnp.float32)
    attended = jnp.einsum('ngtu,und->ngtd', weights, value_head_rows) / row_total[..., None]
    return attended.transpose(2, 0, 1, 3).reshape(sequence_length, QUERY_HEAD_COUNT * HEAD_SIZE).astype(jnp.bfloat16)

def reference(queries, keys, values, resid, out_weight, norm_gain, expert_gate, expert_up, expert_down, route_ids, route_gates):
    attention = lax.map(attend_sequence, (queries, keys, values))
    token_count = SEQUENCE_COUNT * SEQUENCE_LENGTH
    projected = jnp.dot(attention.reshape(token_count, QUERY_HEAD_COUNT * HEAD_SIZE), out_weight, preferred_element_type=jnp.float32)
    attn_resid = (resid.reshape(token_count, D).astype(jnp.float32) + projected).astype(jnp.bfloat16)
    resid_wide = attn_resid.astype(jnp.float32)
    scale_row = lax.rsqrt(lax.optimization_barrier(jnp.mean(resid_wide * resid_wide, axis=-1, keepdims=True)) + norm_eps)
    normed = (resid_wide * scale_row * norm_gain).astype(jnp.bfloat16)
    route_list = route_ids.reshape(token_count, TOPK)
    gate_rows = route_gates.reshape(token_count, TOPK)
    shares = gate_rows / lax.optimization_barrier(jnp.sum(gate_rows, axis=-1, keepdims=True))
    entry_count = token_count * TOPK
    entry_expert = route_list.reshape(entry_count)
    sort_order = jnp.argsort(entry_expert, stable=True).astype(jnp.int32)
    expert_range = jnp.arange(EXPERTS, dtype=jnp.int32)
    counts = lax.optimization_barrier(jnp.sum((entry_expert[:, None] == expert_range[None, :]).astype(jnp.int32), axis=0))
    group_first = jnp.cumsum(counts) - counts
    group_blocks = (counts + tile_height - 1) // tile_height
    block_first = jnp.cumsum(group_blocks) - group_blocks
    sorted_expert = entry_expert[sort_order]
    group_rank = jnp.arange(entry_count, dtype=jnp.int32) - group_first[sorted_expert]
    padded_place = block_first[sorted_expert] * tile_height + group_rank
    block_count = (entry_count + tile_height - 1) // tile_height + EXPERTS
    row_token = jnp.full((block_count * tile_height,), token_count, jnp.int32)
    row_token = row_token.at[padded_place].set(sort_order // TOPK)
    block_index = jnp.arange(block_count, dtype=jnp.int32)
    block_expert = lax.optimization_barrier(jnp.sum((block_first[None, :] <= block_index[:, None]).astype(jnp.int32), axis=1)) - 1
    normed_padded = jnp.concatenate([normed, jnp.zeros((1, D), jnp.bfloat16)], axis=0)

    def run_block(inputs):
        tokens_here, expert_here = inputs
        arrived = normed_padded[tokens_here].astype(jnp.float32)
        gate_part = jnp.dot(arrived, expert_gate[expert_here].astype(jnp.float32))
        up_part = jnp.dot(arrived, expert_up[expert_here].astype(jnp.float32))
        activated = (jax.nn.silu(gate_part) * up_part).astype(jnp.bfloat16)
        return jnp.dot(activated.astype(jnp.float32), expert_down[expert_here].astype(jnp.float32)).astype(jnp.bfloat16)
    block_out = lax.map(run_block, (row_token.reshape(block_count, tile_height), block_expert))
    flat_out = block_out.reshape(block_count * tile_height, D)
    entry_place = jnp.zeros((entry_count,), jnp.int32).at[sort_order].set(padded_place).reshape(token_count, TOPK)
    combined = resid_wide
    for column in range(TOPK):
        combined = combined + shares[:, column:column + 1] * flat_out[entry_place[:, column]].astype(jnp.float32)
    layer_out = combined.astype(jnp.bfloat16)
    return (attn_resid.reshape(SEQUENCE_COUNT, SEQUENCE_LENGTH, D), layer_out.reshape(SEQUENCE_COUNT, SEQUENCE_LENGTH, D))
```

```python
import functools

import jax
import jax.numpy as jnp
from jax import lax
from jax.experimental import pallas as pl
from jax.experimental.pallas import tpu as pltpu
from jax.sharding import PartitionSpec as P

QUERY_HEAD_COUNT = 32
KEY_VALUE_HEADS = 4
HEAD_SIZE = 128
TOPK = 8
CAP = 64

norm_eps = 1e-06
mask_fill_value = -1e30
MIB = 1024 * 1024


def swap(shard, axis, by):
    devices = lax.axis_size(axis)
    return lax.ppermute(shard, axis, [(i, i ^ by) for i in range(devices)])


def dot(a, b):
    return jnp.dot(a, b, preferred_element_type=jnp.float32)


def attention_kernel(blocks, heads, kv_heads, me_ref, *refs):
    ins, out_ref, seq = refs[:blocks], refs[blocks], refs[blocks + 1]
    rows = ins[0].shape[0]
    me = me_ref[0]
    wide = heads * HEAD_SIZE
    for j in range(blocks):
        seq[pl.ds(pl.multiple_of((me ^ j) * rows, rows), rows), :] = ins[j][...]
    row = lax.broadcasted_iota(jnp.int32, (rows, rows), 0)
    col = lax.broadcasted_iota(jnp.int32, (rows, rows), 1)
    allowed = row >= col
    for h in range(heads):
        g = h // (heads // kv_heads)
        key_at = wide + g * HEAD_SIZE
        value_at = wide + (kv_heads + g) * HEAD_SIZE
        for i in range(blocks):
            q = seq[i * rows : (i + 1) * rows, h * HEAD_SIZE : (h + 1) * HEAD_SIZE]
            k = seq[: (i + 1) * rows, key_at : key_at + HEAD_SIZE]
            v = seq[: (i + 1) * rows, value_at : value_at + HEAD_SIZE]
            s = lax.dot_general(
                q, k, (((1,), (1,)), ((), ())), preferred_element_type=jnp.float32
            ) * HEAD_SIZE ** (-0.5)
            last = jnp.where(allowed, s[:, i * rows :], mask_fill_value)
            s = last if i == 0 else jnp.concatenate([s[:, : i * rows], last], axis=1)
            p = jnp.exp(s - jnp.max(s, axis=1, keepdims=True))
            total = jnp.sum(p, axis=1, keepdims=True)
            o = dot(p.astype(jnp.bfloat16), v) / total
            out_ref[
                pl.ds(pl.multiple_of((me ^ i) * rows, rows), rows),
                h * HEAD_SIZE : (h + 1) * HEAD_SIZE,
            ] = o.astype(jnp.bfloat16)


def attention_call(me, ins, heads, kv_heads):
    blocks = len(ins)
    rows, wide_in = ins[0].shape
    length, wide = blocks * rows, heads * HEAD_SIZE
    return pl.pallas_call(
        functools.partial(attention_kernel, blocks, heads, kv_heads),
        out_shape=jax.ShapeDtypeStruct((length, wide), jnp.bfloat16),
        in_specs=[pl.BlockSpec(memory_space=pltpu.SMEM)]
        + [pl.BlockSpec(memory_space=pltpu.VMEM)] * blocks,
        out_specs=pl.BlockSpec(memory_space=pltpu.VMEM),
        scratch_shapes=[pltpu.VMEM((length, wide_in), jnp.bfloat16)],
        compiler_params=pltpu.CompilerParams(vmem_limit_bytes=16 * MIB),
        cost_estimate=pl.CostEstimate(
            flops=4 * length * length * wide,
            bytes_accessed=4 * length * wide_in,
            transcendentals=length * length * heads,
        ),
        name="attention",
    )(me, *ins)


def projection_kernel(pieces, depth, att_ref, *refs):
    ins, outs = refs[:pieces], refs[pieces:]
    rows = outs[0].shape[0]
    piece = ins[0].shape[1]
    for k in range(pieces):
        y = dot(att_ref[...], ins[k][:depth, :]).astype(jnp.bfloat16)
        for j, out in enumerate(outs):
            out[:, k * piece : (k + 1) * piece] = y[j * rows : (j + 1) * rows]


def projection_call(att, packs, blocks):
    length, depth = att.shape
    piece = packs[0].shape[1]
    rows, wide = length // blocks, piece * len(packs)
    return pl.pallas_call(
        functools.partial(projection_kernel, len(packs), depth),
        out_shape=[jax.ShapeDtypeStruct((rows, wide), jnp.bfloat16)] * blocks,
        in_specs=[pl.BlockSpec(memory_space=pltpu.VMEM)] * (1 + len(packs)),
        out_specs=[pl.BlockSpec(memory_space=pltpu.VMEM)] * blocks,
        compiler_params=pltpu.CompilerParams(vmem_limit_bytes=16 * MIB),
        cost_estimate=pl.CostEstimate(
            flops=2 * length * depth * wide,
            bytes_accessed=2 * (length * depth + depth * wide + length * wide),
            transcendentals=0,
        ),
        name="projection",
    )(att, *packs)


def norm_kernel(chunks, blocks, me_ref, resid_ref, gain_ref, *refs):
    parts, (attn_ref, normed_ref) = refs[: chunks * blocks], refs[chunks * blocks :]
    me = me_ref[0]
    width = resid_ref.shape[1]
    wide = parts[0].shape[1]
    pieces = me_ref.shape[0] - 1
    piece = width // pieces
    per = wide // piece
    total = None
    for n in range(chunks):
        for k in range(per):
            at = pl.ds(pl.multiple_of((me ^ (n * per + k)) * piece, piece), piece)
            acc = resid_ref[:, at].astype(jnp.float32)
            for j in range(blocks):
                acc = acc + parts[n * blocks + j][:, k * piece : (k + 1) * piece].astype(
                    jnp.float32
                )
            acc = acc.astype(jnp.bfloat16)
            attn_ref[:, at] = acc
            acc = acc.astype(jnp.float32)
            squares = jnp.sum(acc * acc, axis=1, keepdims=True)
            total = squares if total is None else total + squares
    scale = lax.rsqrt(total / width + norm_eps)
    normed_ref[...] = (attn_ref[...].astype(jnp.float32) * scale * gain_ref[...]).astype(
        jnp.bfloat16
    )


def norm_call(me, resid, gain, parts, blocks, pieces):
    rows, width = resid.shape
    marks = jnp.full((pieces + 1,), me, jnp.int32)
    return pl.pallas_call(
        functools.partial(norm_kernel, len(parts) // blocks, blocks),
        out_shape=[jax.ShapeDtypeStruct((rows, width), jnp.bfloat16)] * 2,
        in_specs=[pl.BlockSpec(memory_space=pltpu.SMEM)]
        + [pl.BlockSpec(memory_space=pltpu.VMEM)] * (2 + len(parts)),
        out_specs=[pl.BlockSpec(memory_space=pltpu.VMEM)] * 2,
        compiler_params=pltpu.CompilerParams(vmem_limit_bytes=16 * MIB),
        cost_estimate=pl.CostEstimate(
            flops=10 * rows * width, bytes_accessed=2 * rows * width * 8, transcendentals=rows
        ),
        name="resid_norm",
    )(marks, resid, gain.reshape(1, width), *parts)


def experts_kernel(sources, local_experts, share_ref, *refs):
    ins = refs[:sources]
    gate_ref, up_ref, down_ref = refs[sources : sources + 3]
    outs = refs[sources + 3 : 2 * sources + 3]
    picked, slot_map, slot_share, acc = refs[2 * sources + 3 :]
    rows = ins[0].shape[0]
    e, f = pl.program_id(0), pl.program_id(1)
    f_last = pl.num_programs(1) - 1

    @pl.when((e == 0) & (f == 0))
    def _():
        before = (
            lax.broadcasted_iota(jnp.int32, (rows, rows), 0)
            < lax.broadcasted_iota(jnp.int32, (rows, rows), 1)
        ).astype(jnp.bfloat16)
        slot = lax.broadcasted_iota(jnp.int32, (CAP, rows), 0).astype(jnp.float32)
        for s in range(sources):
            share = share_ref[s]
            hit = (share > 0.0).astype(jnp.bfloat16)
            rank = dot(hit, before)
            rank = jnp.where(share > 0.0, rank, -1.0)
            for n in range(local_experts):
                taken = slot == rank[n : n + 1, :]
                slot_map[s, n * CAP : (n + 1) * CAP, :] = taken.astype(jnp.bfloat16)
                slot_share[n, s * CAP : (s + 1) * CAP, :] = jnp.sum(
                    jnp.where(taken, share[n : n + 1, :], 0.0), axis=1, keepdims=True
                )
            rows_picked = dot(slot_map[s], ins[s][...]).astype(jnp.bfloat16)
            for n in range(local_experts):
                picked[n, s * CAP : (s + 1) * CAP, :] = rows_picked[n * CAP : (n + 1) * CAP]

    x = picked[e]
    gate_part = dot(x, gate_ref[0])
    up_part = dot(x, up_ref[0])
    activated = gate_part / (1.0 + jnp.exp(-gate_part)) * up_part * slot_share[e]
    y = dot(activated.astype(jnp.bfloat16), down_ref[0])

    @pl.when(f == 0)
    def _():
        acc[e] = y

    @pl.when(f > 0)
    def _():
        acc[e] += y

    @pl.when((e == local_experts - 1) & (f == f_last))
    def _():
        for s in range(sources):
            y_all = jnp.concatenate(
                [acc[n, s * CAP : (s + 1) * CAP, :] for n in range(local_experts)], axis=0
            ).astype(jnp.bfloat16)
            outs[s][...] = lax.dot_general(
                slot_map[s], y_all, (((0,), (0,)), ((), ())), preferred_element_type=jnp.float32
            ).astype(jnp.bfloat16)


def experts_call(share, tokens, gate, up, down, step=256):
    sources = len(tokens)
    rows, width = tokens[0].shape
    local_experts, _, hidden = gate.shape
    slots = sources * CAP
    whole = pl.BlockSpec((rows, width), lambda e, f: (0, 0))
    return pl.pallas_call(
        functools.partial(experts_kernel, sources, local_experts),
        grid=(local_experts, hidden // step),
        out_shape=[jax.ShapeDtypeStruct((rows, width), jnp.bfloat16)] * sources,
        in_specs=[pl.BlockSpec(share.shape, lambda e, f: (0, 0, 0))]
        + [whole] * sources
        + [
            pl.BlockSpec((1, width, step), lambda e, f: (e, 0, f)),
            pl.BlockSpec((1, width, step), lambda e, f: (e, 0, f)),
            pl.BlockSpec((1, step, width), lambda e, f: (e, f, 0)),
        ],
        out_specs=[whole] * sources,
        scratch_shapes=[
            pltpu.VMEM((local_experts, slots, width), jnp.bfloat16),
            pltpu.VMEM((sources, local_experts * CAP, rows), jnp.bfloat16),
            pltpu.VMEM((local_experts, slots, 1), jnp.float32),
            pltpu.VMEM((local_experts, slots, width), jnp.float32),
        ],
        compiler_params=pltpu.CompilerParams(
            vmem_limit_bytes=40 * MIB, dimension_semantics=("arbitrary", "arbitrary")
        ),
        cost_estimate=pl.CostEstimate(
            flops=6 * local_experts * slots * width * hidden,
            bytes_accessed=2 * (3 * local_experts * width * hidden + 2 * sources * rows * width),
            transcendentals=local_experts * slots * hidden,
        ),
        name="experts",
    )(share, *tokens, gate, up, down)


def gather_chips(own, chips):
    same = [own] + [swap(own, "exp", 2 * k) for k in range(1, chips)]
    return [piece for s in same for piece in (s, swap(s, "exp", 1))]


def local(
    queries,
    keys,
    values,
    resid,
    out_weight,
    norm_gain,
    expert_gate,
    expert_up,
    expert_down,
    route_ids,
    route_gates,
):
    rows = queries.shape[1]
    ctx_count = lax.axis_size("ctx")
    exp_count = lax.axis_size("exp")
    chips = exp_count // 2
    ctx_me, exp_me = lax.axis_index("ctx"), lax.axis_index("exp")
    local_experts = expert_gate.shape[0]
    expert_total = local_experts * exp_count
    heads = QUERY_HEAD_COUNT // ctx_count
    group = QUERY_HEAD_COUNT // KEY_VALUE_HEADS
    kv_heads = max(1, heads // group)

    def block_for(who):
        kv_at = who * heads // group * HEAD_SIZE
        return jnp.concatenate(
            [
                lax.dynamic_slice_in_dim(
                    queries[0], who * heads * HEAD_SIZE, heads * HEAD_SIZE, axis=1
                ),
                lax.dynamic_slice_in_dim(keys[0], kv_at, kv_heads * HEAD_SIZE, axis=1),
                lax.dynamic_slice_in_dim(values[0], kv_at, kv_heads * HEAD_SIZE, axis=1),
            ],
            axis=1,
        )

    blocks_in = [block_for(ctx_me)] + [
        swap(block_for(ctx_me ^ j), "ctx", j) for j in range(1, ctx_count)
    ]

    gate_rows = route_gates[0]
    shares = gate_rows / jnp.sum(gate_rows, axis=-1, keepdims=True)
    expert_range = jnp.arange(expert_total, dtype=jnp.int32)
    share_rows = jnp.sum(
        jnp.where(route_ids[0].T[None] == expert_range[:, None, None], shares.T[None], 0.0), axis=1
    )
    share_high = lax.reduce_precision(share_rows, 8, 7)
    share_parts = [share_high.astype(jnp.bfloat16), (share_rows - share_high).astype(jnp.bfloat16)]
    depth, piece = out_weight.shape
    side = 1 if piece >= 2 * rows else 0
    extra = jnp.concatenate(share_parts, axis=side)
    extra = jnp.pad(extra, ((0, 0), (0, piece - extra.shape[1])))
    packs = gather_chips(jnp.concatenate([out_weight, extra], axis=0), chips)

    def share_of(pack):
        both = pack[depth:].astype(jnp.float32)
        if side:
            both = both[:, :rows] + both[:, rows : 2 * rows]
        else:
            both = both[:expert_total, :rows] + both[expert_total:, :rows]
        mine = lax.dynamic_slice_in_dim(both, exp_me * local_experts, local_experts, axis=0)
        return jnp.pad(mine, ((0, 8 - local_experts), (0, 0)))

    share_mine = [share_of(pack) for pack in packs]

    att = attention_call(jnp.full((1,), ctx_me, jnp.int32), blocks_in, heads, kv_heads)

    parts = []
    half = len(packs) // 2
    for some in (packs[:half], packs[half:]):
        mine = projection_call(att, some, ctx_count)
        parts += [mine[0]] + [swap(mine[j], "ctx", j) for j in range(1, ctx_count)]
    attn_resid, normed = norm_call(exp_me, resid[0], norm_gain, parts, ctx_count, exp_count)

    tokens = gather_chips(normed, chips)
    sums = []
    for at in (0, half):
        partial = experts_call(
            jnp.stack(share_mine[at : at + half]),
            tokens[at : at + half],
            expert_gate,
            expert_up,
            expert_down,
        )
        for k in range(0, half, 2):
            both = partial[k].astype(jnp.float32) + swap(partial[k + 1], "exp", 1).astype(
                jnp.float32
            )
            if at + k:
                both = swap(both.astype(jnp.bfloat16), "exp", at + k).astype(jnp.float32)
            sums.append(both)
    layer_out = attn_resid.astype(jnp.float32)
    for s in sums:
        layer_out = layer_out + s
    return (attn_resid[None], layer_out.astype(jnp.bfloat16)[None])


def solution(mesh):
    in_specs = (
        P("exp", "ctx", None),
        P("exp", "ctx", None),
        P("exp", "ctx", None),
        P("exp", "ctx", None),
        P("ctx", "exp"),
        P(),
        P("exp", None, None),
        P("exp", None, None),
        P("exp", None, None),
        P("exp", "ctx", None),
        P("exp", "ctx", None),
    )
    out_specs = (P("exp", "ctx", None), P("exp", "ctx", None))
    return jax.shard_map(local, mesh=mesh, in_specs=in_specs, out_specs=out_specs, check_vma=False)
```

```python
import functools

import jax
import jax.numpy as jnp
from jax import lax
from jax.experimental import pallas as pl
from jax.experimental.pallas import tpu as pltpu
from jax.sharding import PartitionSpec as P

QUERY_HEAD_COUNT = 32
KEY_VALUE_HEADS = 4
HEAD_SIZE = 128
TOPK = 8
CAP = 64

norm_eps = 1e-06
mask_fill_value = -1e30
MIB = 1024 * 1024
VMEM_EXPERTS = 14
VMEM_PREPARE = 58


def swap(shard, axis, by):
    devices = lax.axis_size(axis)
    return lax.ppermute(shard, axis, [(i, i ^ by) for i in range(devices)])


def dot(a, b):
    return jnp.dot(a, b, preferred_element_type=jnp.float32)


def prepare_kernel(blocks, kv_heads, experts, marks_ref, q_ref, k_ref, v_ref, w_ref, ids_ref, gates_ref, *refs):
    outs, pack_ref, sems = refs[:blocks], refs[blocks], refs[blocks + 1]
    rows, width = q_ref.shape
    depth, piece = w_ref.shape
    wide, kv_wide = width // blocks, kv_heads * HEAD_SIZE
    group = QUERY_HEAD_COUNT // KEY_VALUE_HEADS
    copies = []
    for j in list(range(1, blocks)) + [0]:
        who = marks_ref[0] ^ j
        at = pl.ds(pl.multiple_of(who * wide, HEAD_SIZE), wide)
        kv_at = lax.div(who * (wide // HEAD_SIZE), group) * HEAD_SIZE
        kv_at = pl.ds(pl.multiple_of(kv_at, HEAD_SIZE), kv_wide)
        copies += [
            pltpu.make_async_copy(q_ref.at[:, at], outs[j].at[:, :wide], sems.at[3 * j]),
            pltpu.make_async_copy(
                k_ref.at[:, kv_at], outs[j].at[:, wide : wide + kv_wide], sems.at[3 * j + 1]
            ),
            pltpu.make_async_copy(
                v_ref.at[:, kv_at], outs[j].at[:, wide + kv_wide :], sems.at[3 * j + 2]
            ),
        ]
    copies.append(pltpu.make_async_copy(w_ref, pack_ref.at[:depth, :], sems.at[3 * blocks]))
    for copy in copies:
        copy.start()
    gates = gates_ref[...]
    shares = gates / jnp.sum(gates, axis=0, keepdims=True)
    expert = lax.broadcasted_iota(jnp.int32, (experts, rows), 0)
    by_expert = jnp.zeros((experts, rows), jnp.float32)
    for n in range(TOPK):
        by_expert += jnp.where(ids_ref[n : n + 1, :] == expert, shares[n : n + 1, :], 0.0)
    high = by_expert.astype(jnp.bfloat16)
    low = (by_expert - high.astype(jnp.float32)).astype(jnp.bfloat16)
    if piece >= 2 * rows:
        pack_ref[depth:, :rows] = high
        pack_ref[depth:, rows : 2 * rows] = low
    else:
        pack_ref[depth : depth + experts, :rows] = high
        pack_ref[depth + experts :, :rows] = low
    for copy in copies:
        copy.wait()


def prepare_call(marks, q, k, v, w, ids, gates, blocks, kv_heads, experts):
    rows, width = q.shape
    depth, piece = w.shape
    extra = experts if piece >= 2 * rows else 2 * experts
    wide = width // blocks + 2 * kv_heads * HEAD_SIZE
    in_vmem = pl.BlockSpec(memory_space=pltpu.VMEM)
    return pl.pallas_call(
        functools.partial(prepare_kernel, blocks, kv_heads, experts),
        out_shape=[pltpu.VMEM((rows, wide), jnp.bfloat16)] * blocks
        + [pltpu.VMEM((depth + extra, piece), jnp.bfloat16)],
        in_specs=[pl.BlockSpec(memory_space=pltpu.SMEM)]
        + [pl.BlockSpec(memory_space=pltpu.HBM)] * 4
        + [in_vmem] * 2,
        out_specs=[in_vmem] * (blocks + 1),
        scratch_shapes=[pltpu.SemaphoreType.DMA((3 * blocks + 1,))],
        compiler_params=pltpu.CompilerParams(vmem_limit_bytes=VMEM_PREPARE * MIB),
        cost_estimate=pl.CostEstimate(
            flops=rows * experts * 4 * TOPK,
            bytes_accessed=4 * (rows * (width + 4 * kv_heads * HEAD_SIZE) + depth * piece),
            transcendentals=0,
        ),
        name="prepare",
    )(marks, q, k, v, w, ids.T, gates.T)


def attention_kernel(blocks, heads, kv_heads, me_ref, *refs):
    ins, out_ref, seq = refs[:blocks], refs[blocks], refs[blocks + 1]
    rows = ins[0].shape[0]
    me = me_ref[0]
    wide = heads * HEAD_SIZE
    for j in range(blocks):
        seq[pl.ds(pl.multiple_of((me ^ j) * rows, rows), rows), :] = ins[j][...]
    row = lax.broadcasted_iota(jnp.int32, (rows, rows), 0)
    col = lax.broadcasted_iota(jnp.int32, (rows, rows), 1)
    allowed = row >= col
    for h in range(heads):
        g = h // (heads // kv_heads)
        key_at = wide + g * HEAD_SIZE
        value_at = wide + (kv_heads + g) * HEAD_SIZE
        for i in range(blocks):
            q = seq[i * rows : (i + 1) * rows, h * HEAD_SIZE : (h + 1) * HEAD_SIZE]
            k = seq[: (i + 1) * rows, key_at : key_at + HEAD_SIZE]
            v = seq[: (i + 1) * rows, value_at : value_at + HEAD_SIZE]
            s = lax.dot_general(
                q, k, (((1,), (1,)), ((), ())), preferred_element_type=jnp.float32
            ) * HEAD_SIZE ** (-0.5)
            last = jnp.where(allowed, s[:, i * rows :], mask_fill_value)
            s = last if i == 0 else jnp.concatenate([s[:, : i * rows], last], axis=1)
            p = jnp.exp(s - jnp.max(s, axis=1, keepdims=True))
            total = jnp.sum(p, axis=1, keepdims=True)
            o = dot(p.astype(jnp.bfloat16), v) / total
            out_ref[
                pl.ds(pl.multiple_of((me ^ i) * rows, rows), rows),
                h * HEAD_SIZE : (h + 1) * HEAD_SIZE,
            ] = o.astype(jnp.bfloat16)


def attention_call(me, ins, heads, kv_heads):
    blocks = len(ins)
    rows, wide_in = ins[0].shape
    length, wide = blocks * rows, heads * HEAD_SIZE
    return pl.pallas_call(
        functools.partial(attention_kernel, blocks, heads, kv_heads),
        out_shape=jax.ShapeDtypeStruct((length, wide), jnp.bfloat16),
        in_specs=[pl.BlockSpec(memory_space=pltpu.SMEM)]
        + [pl.BlockSpec(memory_space=pltpu.VMEM)] * blocks,
        out_specs=pl.BlockSpec(memory_space=pltpu.VMEM),
        scratch_shapes=[pltpu.VMEM((length, wide_in), jnp.bfloat16)],
        compiler_params=pltpu.CompilerParams(vmem_limit_bytes=12 * MIB),
        cost_estimate=pl.CostEstimate(
            flops=4 * length * length * wide,
            bytes_accessed=4 * length * wide_in,
            transcendentals=length * length * heads,
        ),
        name="attention",
    )(me, *ins)


def projection_kernel(pieces, att_ref, *refs):
    ins, outs = refs[:pieces], refs[pieces:]
    rows = outs[0].shape[0]
    depth = att_ref.shape[1]
    piece = ins[0].shape[1]
    for k in range(pieces):
        y = dot(att_ref[...], ins[k][:depth, :]).astype(jnp.bfloat16)
        for j, out in enumerate(outs):
            out[:, k * piece : (k + 1) * piece] = y[j * rows : (j + 1) * rows]


def projection_call(att, packs, blocks):
    length, depth = att.shape
    piece = packs[0].shape[1]
    rows, wide = length // blocks, piece * len(packs)
    return pl.pallas_call(
        functools.partial(projection_kernel, len(packs)),
        out_shape=[jax.ShapeDtypeStruct((rows, wide), jnp.bfloat16)] * blocks,
        in_specs=[pl.BlockSpec(memory_space=pltpu.VMEM)] * (1 + len(packs)),
        out_specs=[pl.BlockSpec(memory_space=pltpu.VMEM)] * blocks,
        compiler_params=pltpu.CompilerParams(vmem_limit_bytes=8 * MIB),
        cost_estimate=pl.CostEstimate(
            flops=2 * length * depth * wide,
            bytes_accessed=2 * (length * depth + depth * wide + length * wide),
            transcendentals=0,
        ),
        name="projection",
    )(att, *packs)


def norm_kernel(chunks, blocks, piece, me_ref, resid_ref, gain_ref, *refs):
    parts, (attn_ref, normed_ref) = refs[: chunks * blocks], refs[chunks * blocks :]
    me = me_ref[0]
    width = resid_ref.shape[1]
    total = None
    order = 0
    for n in range(chunks):
        for k in range(parts[n * blocks].shape[1] // piece):
            at = pl.ds(pl.multiple_of((me ^ order) * piece, piece), piece)
            order += 1
            acc = resid_ref[:, at].astype(jnp.float32)
            for j in range(blocks):
                acc = acc + parts[n * blocks + j][:, k * piece : (k + 1) * piece].astype(
                    jnp.float32
                )
            acc = acc.astype(jnp.bfloat16)
            attn_ref[:, at] = acc
            acc = acc.astype(jnp.float32)
            squares = jnp.sum(acc * acc, axis=1, keepdims=True)
            total = squares if total is None else total + squares
    scale = lax.rsqrt(total / width + norm_eps)
    normed_ref[...] = (attn_ref[...].astype(jnp.float32) * scale * gain_ref[...]).astype(
        jnp.bfloat16
    )


def norm_call(me, resid, gain, parts, blocks, piece):
    rows, width = resid.shape
    return pl.pallas_call(
        functools.partial(norm_kernel, len(parts) // blocks, blocks, piece),
        out_shape=[jax.ShapeDtypeStruct((rows, width), jnp.bfloat16)] * 2,
        in_specs=[pl.BlockSpec(memory_space=pltpu.SMEM)]
        + [pl.BlockSpec(memory_space=pltpu.VMEM)] * (2 + len(parts)),
        out_specs=[pl.BlockSpec(memory_space=pltpu.VMEM)] * 2,
        compiler_params=pltpu.CompilerParams(vmem_limit_bytes=8 * MIB),
        cost_estimate=pl.CostEstimate(
            flops=10 * rows * width, bytes_accessed=2 * rows * width * 8, transcendentals=rows
        ),
        name="resid_norm",
    )(me, resid, gain.reshape(1, width), *parts)


def experts_kernel(sources, local_experts, step, load, mark_ref, share_ref, *refs):
    ins = refs[:sources]
    weights = refs[sources : sources + 3]
    outs = refs[sources + 3 : 2 * sources + 3]
    refs = refs[2 * sources + 3 :]
    copies = [[] for _ in range(local_experts)]
    if load:
        held, refs, sems = refs[:3], refs[3:-1], refs[-1]
        for n in range(local_experts):
            for m in range(3):
                copy = pltpu.make_async_copy(weights[m].at[n], held[m].at[n], sems.at[n, m])
                copy.start()
                copies[n].append(copy)
        weights = held
    gate_ref, up_ref, down_ref = weights
    picked, slot_map, slot_share, hidden_rows, slot_out = refs
    rows = ins[0].shape[0]
    _, width, hidden = gate_ref.shape
    before = (
        lax.broadcasted_iota(jnp.int32, (rows, rows), 0)
        < lax.broadcasted_iota(jnp.int32, (rows, rows), 1)
    ).astype(jnp.bfloat16)
    slot = lax.broadcasted_iota(jnp.int32, (CAP, rows), 0).astype(jnp.float32)
    for s in range(sources):
        both = share_ref[s].astype(jnp.float32)
        if both.shape[1] >= 2 * rows:
            both = both[:, :rows] + both[:, rows : 2 * rows]
        else:
            both = both[: both.shape[0] // 2, :rows] + both[both.shape[0] // 2 :, :rows]
        expert = lax.broadcasted_iota(jnp.int32, both.shape, 0)
        place = lax.broadcasted_iota(jnp.int32, (8, rows), 0)
        share = jnp.zeros((8, rows), jnp.float32)
        for n in range(local_experts):
            mine = jnp.where(expert == mark_ref[0] * local_experts + n, both, 0.0)
            share = jnp.where(place == n, jnp.sum(mine, axis=0, keepdims=True), share)
        rank = dot((share > 0.0).astype(jnp.bfloat16), before)
        rank = jnp.where(share > 0.0, rank, -1.0)
        for n in range(local_experts):
            taken = slot == rank[n : n + 1, :]
            slot_map[s, n * CAP : (n + 1) * CAP, :] = taken.astype(jnp.bfloat16)
            slot_share[n, s * CAP : (s + 1) * CAP, :] = jnp.sum(
                jnp.where(taken, share[n : n + 1, :], 0.0), axis=1, keepdims=True
            )
        rows_picked = dot(slot_map[s], ins[s][...]).astype(jnp.bfloat16)
        for n in range(local_experts):
            picked[n, s * CAP : (s + 1) * CAP, :] = rows_picked[n * CAP : (n + 1) * CAP]
    for n in range(local_experts):
        for copy in copies[n]:
            copy.wait()
        x = picked[n]
        for at in range(0, hidden, step):
            gate_part = dot(x, gate_ref[n, :, at : at + step])
            up_part = dot(x, up_ref[n, :, at : at + step])
            activated = gate_part / (1.0 + jnp.exp(-gate_part)) * up_part * slot_share[n]
            hidden_rows[:, at : at + step] = activated.astype(jnp.bfloat16)
        for at in range(0, width, 2 * step):
            y = dot(hidden_rows[...], down_ref[n, :, at : at + 2 * step]).astype(jnp.bfloat16)
            for s in range(sources):
                slot_out[s, n * CAP : (n + 1) * CAP, at : at + 2 * step] = y[
                    s * CAP : (s + 1) * CAP
                ]
    for s in range(sources):
        outs[s][...] = lax.dot_general(
            slot_map[s], slot_out[s], (((0,), (0,)), ((), ())), preferred_element_type=jnp.float32
        ).astype(jnp.bfloat16)


def experts_call(mark, share, tokens, weights, load, step=256):
    sources = len(tokens)
    rows, width = tokens[0].shape
    local_experts, _, hidden = weights[0].shape
    slots = sources * CAP
    in_vmem = pl.BlockSpec(memory_space=pltpu.VMEM)
    held = [pltpu.VMEM(w.shape, w.dtype) for w in weights] if load else []
    outs = pl.pallas_call(
        functools.partial(experts_kernel, sources, local_experts, step, load),
        out_shape=[jax.ShapeDtypeStruct((rows, width), jnp.bfloat16)] * sources + held,
        in_specs=[pl.BlockSpec(memory_space=pltpu.SMEM)]
        + [in_vmem] * (sources + 1)
        + [pl.BlockSpec(memory_space=pl.ANY) if load else in_vmem] * 3,
        out_specs=[in_vmem] * (sources + len(held)),
        scratch_shapes=[
            pltpu.VMEM((local_experts, slots, width), jnp.bfloat16),
            pltpu.VMEM((sources, local_experts * CAP, rows), jnp.bfloat16),
            pltpu.VMEM((local_experts, slots, 1), jnp.float32),
            pltpu.VMEM((slots, hidden), jnp.bfloat16),
            pltpu.VMEM((sources, local_experts * CAP, width), jnp.bfloat16),
        ]
        + ([pltpu.SemaphoreType.DMA((local_experts, 3))] if load else []),
        compiler_params=pltpu.CompilerParams(vmem_limit_bytes=VMEM_EXPERTS * MIB),
        cost_estimate=pl.CostEstimate(
            flops=6 * local_experts * slots * width * hidden,
            bytes_accessed=2 * (3 * local_experts * width * hidden + 2 * sources * rows * width),
            transcendentals=local_experts * slots * hidden,
        ),
        name="experts_first" if load else "experts",
    )(mark, share, *tokens, *weights)
    return list(outs[:sources]), list(outs[sources:]) if load else weights


def send_near(own, chips):
    return [swap(own, "exp", 2 * k) for k in range(1, 3 if chips == 4 else chips)]


def send_far(own, near, chips, after):
    if chips != 4:
        return near, after
    two, own, after = lax.optimization_barrier((near[1], own, after))
    relayed = lax.ppermute(two, "exp", [(4, 6), (5, 7), (2, 0), (3, 1)])
    middle = lax.ppermute(own, "exp", [(2, 4), (3, 5), (4, 2), (5, 3)])
    return [near[0], two, (relayed, middle)], after


def take_far(arrays, chips, after):
    far, after = lax.optimization_barrier((arrays[-1], after))
    if chips == 4:
        chip = lax.axis_index("exp") // 2
        far = jnp.where((chip == 0) | (chip == 3), *far)
    return far, after


def local(
    queries,
    keys,
    values,
    resid,
    out_weight,
    norm_gain,
    expert_gate,
    expert_up,
    expert_down,
    route_ids,
    route_gates,
):
    rows = queries.shape[1]
    ctx_count = lax.axis_size("ctx")
    exp_count = lax.axis_size("exp")
    chips = exp_count // 2
    ctx_me, exp_me = lax.axis_index("ctx"), lax.axis_index("exp")
    local_experts = expert_gate.shape[0]
    heads = QUERY_HEAD_COUNT // ctx_count
    group = QUERY_HEAD_COUNT // KEY_VALUE_HEADS
    kv_heads = max(1, heads // group)

    ctx_mark, exp_mark = (jnp.full((1,), me, jnp.int32) for me in (ctx_me, exp_me))
    piece = out_weight.shape[1]

    *blocks_out, pack = prepare_call(
        ctx_mark,
        queries[0],
        keys[0],
        values[0],
        out_weight,
        route_ids[0],
        route_gates[0],
        ctx_count,
        kv_heads,
        local_experts * exp_count,
    )
    pack_chips = send_near(pack, chips)
    blocks_in = blocks_out[:1] + [swap(blocks_out[j], "ctx", j) for j in range(1, ctx_count)]

    att = attention_call(ctx_mark, blocks_in, heads, kv_heads)
    pack_chips, att = send_far(pack, pack_chips, chips, att)

    def project(some):
        mine = projection_call(att, some, ctx_count)
        return [mine[0]] + [swap(mine[j], "ctx", j) for j in range(1, ctx_count)]

    def with_pair(arrays):
        return [both for a in arrays for both in (a, swap(a, "exp", 1))]

    last = chips - 1
    packs = with_pair([pack, pack_chips[0]])
    parts = project(packs)
    middle_packs = with_pair(pack_chips[1 : last - 1])
    parts_middle = project(middle_packs)
    pack_last, (parts, parts_middle[0]) = take_far(pack_chips, chips, (parts, parts_middle[0]))
    packs_last = with_pair([pack_last])
    parts = parts + parts_middle + project(packs_last)
    share = jnp.stack([p[out_weight.shape[0] :] for p in packs + middle_packs + packs_last])
    parts[0], share = lax.optimization_barrier((parts[0], share))
    attn_resid, normed = norm_call(exp_mark, resid[0], norm_gain, parts, ctx_count, piece)

    def experts(which, tokens, weights):
        at = slice(2 * which.start, 2 * which.stop)
        return experts_call(exp_mark, share[at], with_pair(tokens), weights, which.start == 0)

    token_near = send_near(normed, chips)
    partial, weights = experts(
        slice(0, 1), [normed], [expert_gate, expert_up, expert_down]
    )
    token_chips, partial = send_far(normed, token_near, chips, partial)
    token_chips[0], partial[0] = lax.optimization_barrier((token_chips[0], partial[0]))
    more, _ = experts(slice(1, last), token_chips[: last - 1], weights)
    partial = partial + more

    def pair_sum(k):
        return partial[2 * k].astype(jnp.float32) + swap(partial[2 * k + 1], "exp", 1).astype(
            jnp.float32
        )

    layer_out = attn_resid.astype(jnp.float32) + pair_sum(0)
    terms = [swap(pair_sum(k).astype(jnp.bfloat16), "exp", 2 * k) for k in range(1, last)]
    token_last, more = take_far(token_chips, chips, more)
    partial += experts(slice(last, chips), [token_last], weights)[0]
    far, terms = lax.optimization_barrier((pair_sum(last).astype(jnp.bfloat16), terms))
    final = swap(far, "exp", 2 * last)
    for s in terms:
        layer_out = layer_out + s.astype(jnp.float32)
    layer_out = lax.optimization_barrier(layer_out) + final.astype(jnp.float32)
    return (attn_resid[None], layer_out.astype(jnp.bfloat16)[None])


def solution(mesh):
    in_specs = (
        P("exp", "ctx", None),
        P("exp", "ctx", None),
        P("exp", "ctx", None),
        P("exp", "ctx", None),
        P("ctx", "exp"),
        P(),
        P("exp", None, None),
        P("exp", None, None),
        P("exp", None, None),
        P("exp", "ctx", None),
        P("exp", "ctx", None),
    )
    out_specs = (P("exp", "ctx", None), P("exp", "ctx", None))
    return jax.shard_map(local, mesh=mesh, in_specs=in_specs, out_specs=out_specs, check_vma=False)
```

```python
import functools

import jax
import jax.numpy as jnp
from jax import lax
from jax.experimental import pallas as pl
from jax.experimental.pallas import tpu as pltpu
from jax.sharding import PartitionSpec as P

QUERY_HEAD_COUNT = 32
KEY_VALUE_HEADS = 4
HEAD_SIZE = 128
TOPK = 8
CAP = 64

norm_eps = 1e-06
mask_fill_value = -1e30
MIB = 1024 * 1024
VMEM_EXPERTS = 14
VMEM_EXPERTS_FIRST = 32
VMEM_PREPARE = 58


def swap(shard, axis, by):
    devices = lax.axis_size(axis)
    return lax.ppermute(shard, axis, [(i, i ^ by) for i in range(devices)])


def dot(a, b):
    return jnp.dot(a, b, preferred_element_type=jnp.float32)


def prepare_kernel(blocks, kv_heads, experts, marks_ref, q_ref, k_ref, v_ref, w_ref, ids_ref, gates_ref, *refs):
    outs, pack_ref, sems = refs[:blocks], refs[blocks], refs[blocks + 1]
    rows, width = q_ref.shape
    depth, piece = w_ref.shape
    wide, kv_wide = width // blocks, kv_heads * HEAD_SIZE
    group = QUERY_HEAD_COUNT // KEY_VALUE_HEADS
    copies = []
    for j in list(range(1, blocks)) + [0]:
        who = marks_ref[0] ^ j
        at = pl.ds(pl.multiple_of(who * wide, HEAD_SIZE), wide)
        kv_at = lax.div(who * (wide // HEAD_SIZE), group) * HEAD_SIZE
        kv_at = pl.ds(pl.multiple_of(kv_at, HEAD_SIZE), kv_wide)
        copies += [
            pltpu.make_async_copy(q_ref.at[:, at], outs[j].at[:, :wide], sems.at[3 * j]),
            pltpu.make_async_copy(
                k_ref.at[:, kv_at], outs[j].at[:, wide : wide + kv_wide], sems.at[3 * j + 1]
            ),
            pltpu.make_async_copy(
                v_ref.at[:, kv_at], outs[j].at[:, wide + kv_wide :], sems.at[3 * j + 2]
            ),
        ]
    copies.append(pltpu.make_async_copy(w_ref, pack_ref.at[:depth, :], sems.at[3 * blocks]))
    for copy in copies:
        copy.start()
    gates = gates_ref[...]
    shares = gates / jnp.sum(gates, axis=0, keepdims=True)
    expert = lax.broadcasted_iota(jnp.int32, (experts, rows), 0)
    by_expert = jnp.zeros((experts, rows), jnp.float32)
    for n in range(TOPK):
        by_expert += jnp.where(ids_ref[n : n + 1, :] == expert, shares[n : n + 1, :], 0.0)
    high = by_expert.astype(jnp.bfloat16)
    low = (by_expert - high.astype(jnp.float32)).astype(jnp.bfloat16)
    if piece >= 2 * rows:
        pack_ref[depth:, :rows] = high
        pack_ref[depth:, rows : 2 * rows] = low
    else:
        pack_ref[depth : depth + experts, :rows] = high
        pack_ref[depth + experts :, :rows] = low
    for copy in copies:
        copy.wait()


def prepare_call(marks, q, k, v, w, ids, gates, blocks, kv_heads, experts):
    rows, width = q.shape
    depth, piece = w.shape
    extra = experts if piece >= 2 * rows else 2 * experts
    wide = width // blocks + 2 * kv_heads * HEAD_SIZE
    in_vmem = pl.BlockSpec(memory_space=pltpu.VMEM)
    return pl.pallas_call(
        functools.partial(prepare_kernel, blocks, kv_heads, experts),
        out_shape=[pltpu.VMEM((rows, wide), jnp.bfloat16)] * blocks
        + [pltpu.VMEM((depth + extra, piece), jnp.bfloat16)],
        in_specs=[pl.BlockSpec(memory_space=pltpu.SMEM)]
        + [pl.BlockSpec(memory_space=pltpu.HBM)] * 4
        + [in_vmem] * 2,
        out_specs=[in_vmem] * (blocks + 1),
        scratch_shapes=[pltpu.SemaphoreType.DMA((3 * blocks + 1,))],
        compiler_params=pltpu.CompilerParams(vmem_limit_bytes=VMEM_PREPARE * MIB),
        cost_estimate=pl.CostEstimate(
            flops=rows * experts * 4 * TOPK,
            bytes_accessed=4 * (rows * (width + 4 * kv_heads * HEAD_SIZE) + depth * piece),
            transcendentals=0,
        ),
        name="prepare",
    )(marks, q, k, v, w, ids.T, gates.T)


def attention_kernel(blocks, heads, kv_heads, me_ref, *refs):
    ins, out_ref, seq = refs[:blocks], refs[blocks], refs[blocks + 1]
    rows = ins[0].shape[0]
    me = me_ref[0]
    wide = heads * HEAD_SIZE
    for j in range(blocks):
        seq[pl.ds(pl.multiple_of((me ^ j) * rows, rows), rows), :] = ins[j][...]
    row = lax.broadcasted_iota(jnp.int32, (rows, rows), 0)
    col = lax.broadcasted_iota(jnp.int32, (rows, rows), 1)
    allowed = row >= col
    for h in range(heads):
        g = h // (heads // kv_heads)
        key_at = wide + g * HEAD_SIZE
        value_at = wide + (kv_heads + g) * HEAD_SIZE
        for i in range(blocks):
            q = seq[i * rows : (i + 1) * rows, h * HEAD_SIZE : (h + 1) * HEAD_SIZE]
            k = seq[: (i + 1) * rows, key_at : key_at + HEAD_SIZE]
            v = seq[: (i + 1) * rows, value_at : value_at + HEAD_SIZE]
            s = lax.dot_general(
                q, k, (((1,), (1,)), ((), ())), preferred_element_type=jnp.float32
            ) * HEAD_SIZE ** (-0.5)
            last = jnp.where(allowed, s[:, i * rows :], mask_fill_value)
            s = last if i == 0 else jnp.concatenate([s[:, : i * rows], last], axis=1)
            p = jnp.exp(s - jnp.max(s, axis=1, keepdims=True))
            total = jnp.sum(p, axis=1, keepdims=True)
            o = dot(p.astype(jnp.bfloat16), v) / total
            out_ref[
                pl.ds(pl.multiple_of((me ^ i) * rows, rows), rows),
                h * HEAD_SIZE : (h + 1) * HEAD_SIZE,
            ] = o.astype(jnp.bfloat16)


def attention_call(me, ins, heads, kv_heads):
    blocks = len(ins)
    rows, wide_in = ins[0].shape
    length, wide = blocks * rows, heads * HEAD_SIZE
    return pl.pallas_call(
        functools.partial(attention_kernel, blocks, heads, kv_heads),
        out_shape=jax.ShapeDtypeStruct((length, wide), jnp.bfloat16),
        in_specs=[pl.BlockSpec(memory_space=pltpu.SMEM)]
        + [pl.BlockSpec(memory_space=pltpu.VMEM)] * blocks,
        out_specs=pl.BlockSpec(memory_space=pltpu.VMEM),
        scratch_shapes=[pltpu.VMEM((length, wide_in), jnp.bfloat16)],
        compiler_params=pltpu.CompilerParams(vmem_limit_bytes=12 * MIB),
        cost_estimate=pl.CostEstimate(
            flops=4 * length * length * wide,
            bytes_accessed=4 * length * wide_in,
            transcendentals=length * length * heads,
        ),
        name="attention",
    )(me, *ins)


def projection_kernel(pieces, att_ref, *refs):
    ins, outs = refs[:pieces], refs[pieces:]
    rows = outs[0].shape[0]
    depth = att_ref.shape[1]
    piece = ins[0].shape[1]
    for k in range(pieces):
        y = dot(att_ref[...], ins[k][:depth, :]).astype(jnp.bfloat16)
        for j, out in enumerate(outs):
            out[:, k * piece : (k + 1) * piece] = y[j * rows : (j + 1) * rows]


def projection_call(att, packs, blocks):
    length, depth = att.shape
    piece = packs[0].shape[1]
    rows, wide = length // blocks, piece * len(packs)
    return pl.pallas_call(
        functools.partial(projection_kernel, len(packs)),
        out_shape=[jax.ShapeDtypeStruct((rows, wide), jnp.bfloat16)] * blocks,
        in_specs=[pl.BlockSpec(memory_space=pltpu.VMEM)] * (1 + len(packs)),
        out_specs=[pl.BlockSpec(memory_space=pltpu.VMEM)] * blocks,
        compiler_params=pltpu.CompilerParams(vmem_limit_bytes=8 * MIB),
        cost_estimate=pl.CostEstimate(
            flops=2 * length * depth * wide,
            bytes_accessed=2 * (length * depth + depth * wide + length * wide),
            transcendentals=0,
        ),
        name="projection",
    )(att, *packs)


def norm_kernel(chunks, blocks, piece, me_ref, resid_ref, gain_ref, *refs):
    parts, (attn_ref, normed_ref) = refs[: chunks * blocks], refs[chunks * blocks :]
    me = me_ref[0]
    width = resid_ref.shape[1]
    total = None
    order = 0
    for n in range(chunks):
        for k in range(parts[n * blocks].shape[1] // piece):
            at = pl.ds(pl.multiple_of((me ^ order) * piece, piece), piece)
            order += 1
            acc = resid_ref[:, at].astype(jnp.float32)
            for j in range(blocks):
                acc = acc + parts[n * blocks + j][:, k * piece : (k + 1) * piece].astype(
                    jnp.float32
                )
            acc = acc.astype(jnp.bfloat16)
            attn_ref[:, at] = acc
            acc = acc.astype(jnp.float32)
            squares = jnp.sum(acc * acc, axis=1, keepdims=True)
            total = squares if total is None else total + squares
    scale = lax.rsqrt(total / width + norm_eps)
    normed_ref[...] = (attn_ref[...].astype(jnp.float32) * scale * gain_ref[...]).astype(
        jnp.bfloat16
    )


def norm_call(me, resid, gain, parts, blocks, piece):
    rows, width = resid.shape
    return pl.pallas_call(
        functools.partial(norm_kernel, len(parts) // blocks, blocks, piece),
        out_shape=[jax.ShapeDtypeStruct((rows, width), jnp.bfloat16)] * 2,
        in_specs=[pl.BlockSpec(memory_space=pltpu.SMEM)]
        + [pl.BlockSpec(memory_space=pltpu.VMEM)] * (2 + len(parts)),
        out_specs=[pl.BlockSpec(memory_space=pltpu.VMEM)] * 2,
        compiler_params=pltpu.CompilerParams(vmem_limit_bytes=8 * MIB),
        cost_estimate=pl.CostEstimate(
            flops=10 * rows * width, bytes_accessed=2 * rows * width * 8, transcendentals=rows
        ),
        name="resid_norm",
    )(me, resid, gain.reshape(1, width), *parts)


def experts_kernel(sources, local_experts, step, load, mark_ref, share_ref, *refs):
    ins = refs[:sources]
    weights = refs[sources : sources + 3]
    outs = refs[sources + 3 : 2 * sources + 3]
    refs[2 * sources + 3][0] = mark_ref[0]
    refs = refs[2 * sources + 4 :]
    copies = [[] for _ in range(local_experts)]
    if load:
        held, refs, sems = refs[:3], refs[3:-1], refs[-1]
        for n in range(local_experts):
            for m in range(3):
                copy = pltpu.make_async_copy(weights[m].at[n], held[m].at[n], sems.at[n, m])
                copy.start()
                copies[n].append(copy)
        weights = held
    gate_ref, up_ref, down_ref = weights
    picked, slot_map, slot_share, hidden_rows, slot_out = refs
    rows = ins[0].shape[0]
    _, width, hidden = gate_ref.shape
    before = (
        lax.broadcasted_iota(jnp.int32, (rows, rows), 0)
        < lax.broadcasted_iota(jnp.int32, (rows, rows), 1)
    ).astype(jnp.bfloat16)
    slot = lax.broadcasted_iota(jnp.int32, (CAP, rows), 0).astype(jnp.float32)
    for s in range(sources):
        both = share_ref[s].astype(jnp.float32)
        if both.shape[1] >= 2 * rows:
            both = both[:, :rows] + both[:, rows : 2 * rows]
        else:
            both = both[: both.shape[0] // 2, :rows] + both[both.shape[0] // 2 :, :rows]
        expert = lax.broadcasted_iota(jnp.int32, both.shape, 0)
        place = lax.broadcasted_iota(jnp.int32, (8, rows), 0)
        share = jnp.zeros((8, rows), jnp.float32)
        for n in range(local_experts):
            mine = jnp.where(expert == mark_ref[0] * local_experts + n, both, 0.0)
            share = jnp.where(place == n, jnp.sum(mine, axis=0, keepdims=True), share)
        rank = dot((share > 0.0).astype(jnp.bfloat16), before)
        rank = jnp.where(share > 0.0, rank, -1.0)
        for n in range(local_experts):
            taken = slot == rank[n : n + 1, :]
            slot_map[s, n * CAP : (n + 1) * CAP, :] = taken.astype(jnp.bfloat16)
            slot_share[n, s * CAP : (s + 1) * CAP, :] = jnp.sum(
                jnp.where(taken, share[n : n + 1, :], 0.0), axis=1, keepdims=True
            )
        rows_picked = dot(slot_map[s], ins[s][...]).astype(jnp.bfloat16)
        for n in range(local_experts):
            picked[n, s * CAP : (s + 1) * CAP, :] = rows_picked[n * CAP : (n + 1) * CAP]
    for n in range(local_experts):
        for copy in copies[n]:
            copy.wait()
        x = picked[n]
        for at in range(0, hidden, step):
            gate_part = dot(x, gate_ref[n, :, at : at + step])
            up_part = dot(x, up_ref[n, :, at : at + step])
            activated = gate_part / (1.0 + jnp.exp(-gate_part)) * up_part * slot_share[n]
            hidden_rows[:, at : at + step] = activated.astype(jnp.bfloat16)
        for at in range(0, width, 2 * step):
            y = dot(hidden_rows[...], down_ref[n, :, at : at + 2 * step]).astype(jnp.bfloat16)
            for s in range(sources):
                slot_out[s, n * CAP : (n + 1) * CAP, at : at + 2 * step] = y[
                    s * CAP : (s + 1) * CAP
                ]
    for s in range(sources):
        outs[s][...] = lax.dot_general(
            slot_map[s], slot_out[s], (((0,), (0,)), ((), ())), preferred_element_type=jnp.float32
        ).astype(jnp.bfloat16)


def experts_call(mark, share, tokens, weights, load, step=256):
    sources = len(tokens)
    rows, width = tokens[0].shape
    local_experts, _, hidden = weights[0].shape
    slots = sources * CAP
    in_vmem = pl.BlockSpec(memory_space=pltpu.VMEM)
    held = [pltpu.VMEM(w.shape, w.dtype) for w in weights] if load else []
    outs = pl.pallas_call(
        functools.partial(experts_kernel, sources, local_experts, step, load),
        out_shape=[jax.ShapeDtypeStruct((rows, width), jnp.bfloat16)] * sources
        + [jax.ShapeDtypeStruct((1,), jnp.int32)]
        + held,
        in_specs=[pl.BlockSpec(memory_space=pltpu.SMEM)]
        + [in_vmem] * (sources + 1)
        + [pl.BlockSpec(memory_space=pl.ANY) if load else in_vmem] * 3,
        out_specs=[in_vmem] * sources
        + [pl.BlockSpec(memory_space=pltpu.SMEM)]
        + [in_vmem] * len(held),
        scratch_shapes=[
            pltpu.VMEM((local_experts, slots, width), jnp.bfloat16),
            pltpu.VMEM((sources, local_experts * CAP, rows), jnp.bfloat16),
            pltpu.VMEM((local_experts, slots, 1), jnp.float32),
            pltpu.VMEM((slots, hidden), jnp.bfloat16),
            pltpu.VMEM((sources, local_experts * CAP, width), jnp.bfloat16),
        ]
        + ([pltpu.SemaphoreType.DMA((local_experts, 3))] if load else []),
        compiler_params=pltpu.CompilerParams(vmem_limit_bytes=(VMEM_EXPERTS_FIRST if load else VMEM_EXPERTS) * MIB),
        cost_estimate=pl.CostEstimate(
            flops=6 * local_experts * slots * width * hidden,
            bytes_accessed=2 * (3 * local_experts * width * hidden + 2 * sources * rows * width),
            transcendentals=local_experts * slots * hidden,
        ),
        name="experts_first" if load else "experts",
    )(mark, share, *tokens, *weights)
    return list(outs[:sources]), outs[sources], list(outs[sources + 1 :]) if load else weights


def over_line(array, pairs):
    return lax.ppermute(array, "exp", [(2 * a + c, 2 * b + c) for a, b in pairs for c in (0, 1)])


def pick_kernel(mark_ref, relayed_ref, middle_ref, out_ref):
    chip = lax.div(mark_ref[0], 2)
    at_end = (chip == 0) | (chip == 3)

    @pl.when(at_end)
    def _():
        out_ref[...] = relayed_ref[...]

    @pl.when(jnp.logical_not(at_end))
    def _():
        out_ref[...] = middle_ref[...]


def take_far(far, mark, chips):
    if chips != 4:
        return lax.optimization_barrier((far, mark))[0]
    in_vmem = pl.BlockSpec(memory_space=pltpu.VMEM)
    return pl.pallas_call(
        pick_kernel,
        out_shape=jax.ShapeDtypeStruct(far[0].shape, far[0].dtype),
        in_specs=[pl.BlockSpec(memory_space=pltpu.SMEM)] + [in_vmem] * 2,
        out_specs=in_vmem,
        compiler_params=pltpu.CompilerParams(vmem_limit_bytes=4 * MIB),
        cost_estimate=pl.CostEstimate(flops=0, bytes_accessed=6 * far[0].size, transcendentals=0),
        name="pick_far",
    )(mark, *far)


def local(
    queries,
    keys,
    values,
    resid,
    out_weight,
    norm_gain,
    expert_gate,
    expert_up,
    expert_down,
    route_ids,
    route_gates,
):
    rows = queries.shape[1]
    ctx_count = lax.axis_size("ctx")
    exp_count = lax.axis_size("exp")
    chips = exp_count // 2
    ctx_me, exp_me = lax.axis_index("ctx"), lax.axis_index("exp")
    local_experts = expert_gate.shape[0]
    heads = QUERY_HEAD_COUNT // ctx_count
    group = QUERY_HEAD_COUNT // KEY_VALUE_HEADS
    kv_heads = max(1, heads // group)

    ctx_mark, exp_mark = (jnp.full((1,), me, jnp.int32) for me in (ctx_me, exp_me))
    piece = out_weight.shape[1]

    *blocks_out, pack = prepare_call(
        ctx_mark,
        queries[0],
        keys[0],
        values[0],
        out_weight,
        route_ids[0],
        route_gates[0],
        ctx_count,
        kv_heads,
        local_experts * exp_count,
    )
    blocks_in = blocks_out[:1] + [swap(blocks_out[j], "ctx", j) for j in range(1, ctx_count)]
    last = chips - 1
    pack_chips = [swap(pack, "exp", 2 * k) for k in range(1, last)]

    att = attention_call(ctx_mark, blocks_in, heads, kv_heads)
    pack_mine, pack_chips[0], att = lax.optimization_barrier((pack, pack_chips[0], att))
    if chips == 4:
        two, pack_mine, att = lax.optimization_barrier((pack_chips[1], pack_mine, att))
        pack_chips[1] = two
        pack_far = (
            over_line(two, [(2, 3), (1, 0)]),
            over_line(pack_mine, [(1, 2), (2, 1)]),
        )
    else:
        pack_far = swap(pack, "exp", 2 * last)

    def project(some):
        mine = projection_call(att, some, ctx_count)
        return [mine[0]] + [swap(mine[j], "ctx", j) for j in range(1, ctx_count)]

    def with_pair(arrays):
        return [both for a in arrays for both in (a, swap(a, "exp", 1))]

    packs = with_pair([pack_mine, pack_chips[0]])
    parts = project(packs)
    packs_middle = with_pair(pack_chips[1:])
    parts_middle = project(packs_middle)
    pack_far, parts, parts_middle[0] = lax.optimization_barrier((pack_far, parts, parts_middle[0]))
    packs_last = with_pair([take_far(pack_far, exp_mark, chips)])
    parts = parts + parts_middle + project(packs_last)
    share = jnp.stack([p[out_weight.shape[0] :] for p in packs + packs_middle + packs_last])
    parts[0], share = lax.optimization_barrier((parts[0], share))
    attn_resid, normed = norm_call(exp_mark, resid[0], norm_gain, parts, ctx_count, piece)

    def experts(which, mark, tokens, weights):
        at = slice(2 * which.start, 2 * which.stop)
        return experts_call(mark, share[at], with_pair(tokens), weights, which.start == 0)

    def pair_sum(both):
        return both[0].astype(jnp.float32) + swap(both[1], "exp", 1).astype(jnp.float32)

    near = [swap(normed, "exp", 2 * k) for k in range(1, last)]
    partial, mark, weights = experts(
        slice(0, 1), exp_mark, [normed], [expert_gate, expert_up, expert_down]
    )
    if chips == 4:
        near[1], normed, mark = lax.optimization_barrier((near[1], normed, mark))
        far = (
            over_line(near[1], [(2, 3), (1, 0)]),
            over_line(normed, [(1, 2), (2, 1)]),
        )
    else:
        far = swap(normed, "exp", 2 * last)
    layer_out = attn_resid.astype(jnp.float32) + pair_sum(partial)
    partial, mark, _ = experts(slice(1, last), mark, near, weights)
    sums = [pair_sum(partial[2 * k :]).astype(jnp.bfloat16) for k in range(last - 1)]
    partial, _, _ = experts(slice(last, chips), mark, [take_far(far, mark, chips)], weights)
    sum_far = pair_sum(partial).astype(jnp.bfloat16)
    if chips == 4:
        relayed = over_line(sum_far, [(3, 2), (0, 1)])
        terms = [swap(sums[0], "exp", 2), over_line(sum_far, [(1, 2), (2, 1)])]
        both = sums[1].astype(jnp.float32) + relayed.astype(jnp.float32)
        final = swap(both.astype(jnp.bfloat16), "exp", 4)
    else:
        terms = [swap(p, "exp", 2 * k) for k, p in enumerate(sums, 1)]
        final = swap(sum_far, "exp", 2 * last)
    for s in terms:
        layer_out = layer_out + s.astype(jnp.float32)
    layer_out = lax.optimization_barrier(layer_out) + final.astype(jnp.float32)
    return (attn_resid[None], layer_out.astype(jnp.bfloat16)[None])


def solution(mesh):
    in_specs = (
        P("exp", "ctx", None),
        P("exp", "ctx", None),
        P("exp", "ctx", None),
        P("exp", "ctx", None),
        P("ctx", "exp"),
        P(),
        P("exp", None, None),
        P("exp", None, None),
        P("exp", None, None),
        P("exp", "ctx", None),
        P("exp", "ctx", None),
    )
    out_specs = (P("exp", "ctx", None), P("exp", "ctx", None))
    return jax.shard_map(local, mesh=mesh, in_specs=in_specs, out_specs=out_specs, check_vma=False)
```

```python
import functools
import math

import jax
import jax.numpy as jnp
from jax import lax
from jax.experimental import pallas as pl
from jax.experimental.pallas import tpu as pltpu
from jax.sharding import PartitionSpec as P

QUERY_HEAD_COUNT = 32
KEY_VALUE_HEADS = 4
HEAD_SIZE = 128
TOPK = 8
CAP = 64

norm_eps = 1e-06
mask_fill_value = -1e30
MIB = 1024 * 1024
VMEM_EXPERTS = 14
VMEM_EXPERTS_FIRST = 32
VMEM_PREPARE = 58


def swap(shard, axis, by):
    devices = lax.axis_size(axis)
    return lax.ppermute(shard, axis, [(i, i ^ by) for i in range(devices)])


def dot(a, b):
    return jnp.dot(a, b, preferred_element_type=jnp.float32)


def prepare_kernel(blocks, kv_heads, experts, marks_ref, q_ref, k_ref, v_ref, w_ref, ids_ref, gates_ref, *refs):
    outs, pack_ref, sems = refs[:blocks], refs[blocks], refs[blocks + 1]
    rows, width = q_ref.shape
    depth, piece = w_ref.shape
    wide, kv_wide = width // blocks, kv_heads * HEAD_SIZE
    group = QUERY_HEAD_COUNT // KEY_VALUE_HEADS
    copies = []
    for j in list(range(1, blocks)) + [0]:
        who = marks_ref[0] ^ j
        at = pl.ds(pl.multiple_of(who * wide, HEAD_SIZE), wide)
        kv_at = lax.div(who * (wide // HEAD_SIZE), group) * HEAD_SIZE
        kv_at = pl.ds(pl.multiple_of(kv_at, HEAD_SIZE), kv_wide)
        copies += [
            pltpu.make_async_copy(q_ref.at[:, at], outs[j].at[:, :wide], sems.at[3 * j]),
            pltpu.make_async_copy(
                k_ref.at[:, kv_at], outs[j].at[:, wide : wide + kv_wide], sems.at[3 * j + 1]
            ),
            pltpu.make_async_copy(
                v_ref.at[:, kv_at], outs[j].at[:, wide + kv_wide :], sems.at[3 * j + 2]
            ),
        ]
    copies.append(pltpu.make_async_copy(w_ref, pack_ref.at[:depth, :], sems.at[3 * blocks]))
    for copy in copies:
        copy.start()
    gates = gates_ref[...]
    shares = gates / jnp.sum(gates, axis=0, keepdims=True)
    expert = lax.broadcasted_iota(jnp.int32, (experts, rows), 0)
    by_expert = jnp.zeros((experts, rows), jnp.float32)
    for n in range(TOPK):
        by_expert += jnp.where(ids_ref[n : n + 1, :] == expert, shares[n : n + 1, :], 0.0)
    high = by_expert.astype(jnp.bfloat16)
    low = (by_expert - high.astype(jnp.float32)).astype(jnp.bfloat16)
    if piece >= 2 * rows:
        pack_ref[depth:, :rows] = high
        pack_ref[depth:, rows : 2 * rows] = low
    else:
        pack_ref[depth : depth + experts, :rows] = high
        pack_ref[depth + experts :, :rows] = low
    for copy in copies:
        copy.wait()


def prepare_call(marks, q, k, v, w, ids, gates, blocks, kv_heads, experts):
    rows, width = q.shape
    depth, piece = w.shape
    extra = experts if piece >= 2 * rows else 2 * experts
    wide = width // blocks + 2 * kv_heads * HEAD_SIZE
    in_vmem = pl.BlockSpec(memory_space=pltpu.VMEM)
    return pl.pallas_call(
        functools.partial(prepare_kernel, blocks, kv_heads, experts),
        out_shape=[pltpu.VMEM((rows, wide), jnp.bfloat16)] * blocks
        + [pltpu.VMEM((depth + extra, piece), jnp.bfloat16)],
        in_specs=[pl.BlockSpec(memory_space=pltpu.SMEM)]
        + [pl.BlockSpec(memory_space=pltpu.HBM)] * 4
        + [in_vmem] * 2,
        out_specs=[in_vmem] * (blocks + 1),
        scratch_shapes=[pltpu.SemaphoreType.DMA((3 * blocks + 1,))],
        compiler_params=pltpu.CompilerParams(vmem_limit_bytes=VMEM_PREPARE * MIB),
        cost_estimate=pl.CostEstimate(
            flops=rows * experts * 4 * TOPK,
            bytes_accessed=4 * (rows * (width + 4 * kv_heads * HEAD_SIZE) + depth * piece),
            transcendentals=0,
        ),
        name="prepare",
    )(marks, q, k, v, w, ids.T, gates.T)


STACK = 4


def attention_kernel(blocks, heads, kv_heads, me_ref, *refs):
    ins, out_ref = refs[:blocks], refs[blocks]
    query_rows, key_rows, value_rows = refs[blocks + 1 :]
    rows = ins[0].shape[0]
    me = me_ref[0]
    wide = heads * HEAD_SIZE
    value_rows[:, :, HEAD_SIZE:] = jnp.ones(value_rows.shape[:2] + (HEAD_SIZE,), jnp.bfloat16)
    for j in range(blocks):
        at = pl.ds(pl.multiple_of((me ^ j) * rows, rows), rows)
        for h in range(heads):
            query_rows[h, at, :] = ins[j][:, h * HEAD_SIZE : (h + 1) * HEAD_SIZE]
        for g in range(kv_heads):
            key_at, value_at = wide + g * HEAD_SIZE, wide + (kv_heads + g) * HEAD_SIZE
            key_rows[g, at, :] = ins[j][:, key_at : key_at + HEAD_SIZE]
            value_rows[g, at, :HEAD_SIZE] = ins[j][:, value_at : value_at + HEAD_SIZE]
    group = heads // kv_heads
    stack = min(STACK, group)
    row = lax.broadcasted_iota(jnp.int32, (rows, rows), 0)
    col = lax.broadcasted_iota(jnp.int32, (rows, rows), 1)
    allowed = jnp.concatenate([row >= col] * stack, axis=0)
    factor = HEAD_SIZE ** (-0.5) * math.log2(math.e)
    for h in range(0, heads, stack):
        g = h // group
        for i in range(blocks):
            q = query_rows[h : h + stack, i * rows : (i + 1) * rows, :]
            s = lax.dot_general(
                q.reshape(stack * rows, HEAD_SIZE),
                key_rows[g, : (i + 1) * rows, :],
                (((1,), (1,)), ((), ())),
                preferred_element_type=jnp.float32,
            )
            last = jnp.where(allowed, s[:, i * rows :], mask_fill_value)
            s = last if i == 0 else jnp.concatenate([s[:, : i * rows], last], axis=1)
            p = jnp.exp2((s - jnp.max(s, axis=1, keepdims=True)) * factor)
            o = dot(p.astype(jnp.bfloat16), value_rows[g, : (i + 1) * rows, :])
            o = (o[:, :HEAD_SIZE] / o[:, HEAD_SIZE:]).astype(jnp.bfloat16)
            at = pl.ds(pl.multiple_of((me ^ i) * rows, rows), rows)
            for n in range(stack):
                out_ref[at, (h + n) * HEAD_SIZE : (h + n + 1) * HEAD_SIZE] = o[
                    n * rows : (n + 1) * rows
                ]


def attention_call(me, ins, heads, kv_heads):
    blocks = len(ins)
    rows, wide_in = ins[0].shape
    length, wide = blocks * rows, heads * HEAD_SIZE
    return pl.pallas_call(
        functools.partial(attention_kernel, blocks, heads, kv_heads),
        out_shape=jax.ShapeDtypeStruct((length, wide), jnp.bfloat16),
        in_specs=[pl.BlockSpec(memory_space=pltpu.SMEM)]
        + [pl.BlockSpec(memory_space=pltpu.VMEM)] * blocks,
        out_specs=pl.BlockSpec(memory_space=pltpu.VMEM),
        scratch_shapes=[
            pltpu.VMEM((heads, length, HEAD_SIZE), jnp.bfloat16),
            pltpu.VMEM((kv_heads, length, HEAD_SIZE), jnp.bfloat16),
            pltpu.VMEM((kv_heads, length, 2 * HEAD_SIZE), jnp.bfloat16),
        ],
        compiler_params=pltpu.CompilerParams(vmem_limit_bytes=24 * MIB),
        cost_estimate=pl.CostEstimate(
            flops=4 * length * length * wide,
            bytes_accessed=4 * length * wide_in,
            transcendentals=length * length * heads,
        ),
        name="attention",
    )(me, *ins)


def projection_kernel(pieces, att_ref, *refs):
    ins, outs = refs[:pieces], refs[pieces:]
    rows = outs[0].shape[0]
    depth = att_ref.shape[1]
    piece = ins[0].shape[1]
    for k in range(pieces):
        y = dot(att_ref[...], ins[k][:depth, :]).astype(jnp.bfloat16)
        for j, out in enumerate(outs):
            out[:, k * piece : (k + 1) * piece] = y[j * rows : (j + 1) * rows]


def projection_call(att, packs, blocks):
    length, depth = att.shape
    piece = packs[0].shape[1]
    rows, wide = length // blocks, piece * len(packs)
    return pl.pallas_call(
        functools.partial(projection_kernel, len(packs)),
        out_shape=[jax.ShapeDtypeStruct((rows, wide), jnp.bfloat16)] * blocks,
        in_specs=[pl.BlockSpec(memory_space=pltpu.VMEM)] * (1 + len(packs)),
        out_specs=[pl.BlockSpec(memory_space=pltpu.VMEM)] * blocks,
        compiler_params=pltpu.CompilerParams(vmem_limit_bytes=8 * MIB),
        cost_estimate=pl.CostEstimate(
            flops=2 * length * depth * wide,
            bytes_accessed=2 * (length * depth + depth * wide + length * wide),
            transcendentals=0,
        ),
        name="projection",
    )(att, *packs)


def norm_kernel(chunks, blocks, piece, me_ref, resid_ref, gain_ref, *refs):
    parts, (attn_ref, normed_ref) = refs[: chunks * blocks], refs[chunks * blocks :]
    me = me_ref[0]
    width = resid_ref.shape[1]
    total = None
    order = 0
    for n in range(chunks):
        for k in range(parts[n * blocks].shape[1] // piece):
            at = pl.ds(pl.multiple_of((me ^ order) * piece, piece), piece)
            order += 1
            acc = resid_ref[:, at].astype(jnp.float32)
            for j in range(blocks):
                acc = acc + parts[n * blocks + j][:, k * piece : (k + 1) * piece].astype(
                    jnp.float32
                )
            acc = acc.astype(jnp.bfloat16)
            attn_ref[:, at] = acc
            acc = acc.astype(jnp.float32)
            squares = jnp.sum(acc * acc, axis=1, keepdims=True)
            total = squares if total is None else total + squares
    scale = lax.rsqrt(total / width + norm_eps)
    normed_ref[...] = (attn_ref[...].astype(jnp.float32) * scale * gain_ref[...]).astype(
        jnp.bfloat16
    )


def norm_call(me, resid, gain, parts, blocks, piece):
    rows, width = resid.shape
    return pl.pallas_call(
        functools.partial(norm_kernel, len(parts) // blocks, blocks, piece),
        out_shape=[jax.ShapeDtypeStruct((rows, width), jnp.bfloat16)] * 2,
        in_specs=[pl.BlockSpec(memory_space=pltpu.SMEM)]
        + [pl.BlockSpec(memory_space=pltpu.VMEM)] * (2 + len(parts)),
        out_specs=[pl.BlockSpec(memory_space=pltpu.VMEM)] * 2,
        compiler_params=pltpu.CompilerParams(vmem_limit_bytes=8 * MIB),
        cost_estimate=pl.CostEstimate(
            flops=10 * rows * width, bytes_accessed=2 * rows * width * 8, transcendentals=rows
        ),
        name="resid_norm",
    )(me, resid, gain.reshape(1, width), *parts)


def experts_kernel(sources, local_experts, step, load, mark_ref, share_ref, *refs):
    ins = refs[:sources]
    weights = refs[sources : sources + 3]
    outs = refs[sources + 3 : 2 * sources + 3]
    refs[2 * sources + 3][0] = mark_ref[0]
    refs = refs[2 * sources + 4 :]
    copies = [[] for _ in range(local_experts)]
    if load:
        held, refs, sems = refs[:3], refs[3:-1], refs[-1]
        for n in range(local_experts):
            for m in range(3):
                copy = pltpu.make_async_copy(weights[m].at[n], held[m].at[n], sems.at[n, m])
                copy.start()
                copies[n].append(copy)
        weights = held
    gate_ref, up_ref, down_ref = weights
    picked, slot_map, slot_share, hidden_rows, slot_out = refs
    rows = ins[0].shape[0]
    _, width, hidden = gate_ref.shape
    before = (
        lax.broadcasted_iota(jnp.int32, (rows, rows), 0)
        < lax.broadcasted_iota(jnp.int32, (rows, rows), 1)
    ).astype(jnp.bfloat16)
    slot = lax.broadcasted_iota(jnp.int32, (CAP, rows), 0).astype(jnp.float32)
    for s in range(sources):
        both = share_ref[s].astype(jnp.float32)
        if both.shape[1] >= 2 * rows:
            both = both[:, :rows] + both[:, rows : 2 * rows]
        else:
            both = both[: both.shape[0] // 2, :rows] + both[both.shape[0] // 2 :, :rows]
        expert = lax.broadcasted_iota(jnp.int32, both.shape, 0)
        place = lax.broadcasted_iota(jnp.int32, (8, rows), 0)
        share = jnp.zeros((8, rows), jnp.float32)
        for n in range(local_experts):
            mine = jnp.where(expert == mark_ref[0] * local_experts + n, both, 0.0)
            share = jnp.where(place == n, jnp.sum(mine, axis=0, keepdims=True), share)
        rank = dot((share > 0.0).astype(jnp.bfloat16), before)
        rank = jnp.where(share > 0.0, rank, -1.0)
        for n in range(local_experts):
            taken = slot == rank[n : n + 1, :]
            slot_map[s, n * CAP : (n + 1) * CAP, :] = taken.astype(jnp.bfloat16)
            slot_share[n, s * CAP : (s + 1) * CAP, :] = jnp.sum(
                jnp.where(taken, share[n : n + 1, :], 0.0), axis=1, keepdims=True
            )
        rows_picked = dot(slot_map[s], ins[s][...]).astype(jnp.bfloat16)
        for n in range(local_experts):
            picked[n, s * CAP : (s + 1) * CAP, :] = rows_picked[n * CAP : (n + 1) * CAP]
    for n in range(local_experts):
        for copy in copies[n]:
            copy.wait()
        x = picked[n]
        for at in range(0, hidden, step):
            gate_part = dot(x, gate_ref[n, :, at : at + step])
            up_part = dot(x, up_ref[n, :, at : at + step])
            activated = gate_part / (1.0 + jnp.exp(-gate_part)) * up_part * slot_share[n]
            hidden_rows[:, at : at + step] = activated.astype(jnp.bfloat16)
        for at in range(0, width, 2 * step):
            y = dot(hidden_rows[...], down_ref[n, :, at : at + 2 * step]).astype(jnp.bfloat16)
            for s in range(sources):
                slot_out[s, n * CAP : (n + 1) * CAP, at : at + 2 * step] = y[
                    s * CAP : (s + 1) * CAP
                ]
    for s in range(sources):
        outs[s][...] = lax.dot_general(
            slot_map[s], slot_out[s], (((0,), (0,)), ((), ())), preferred_element_type=jnp.float32
        ).astype(jnp.bfloat16)


def experts_call(mark, share, tokens, weights, load, step=256):
    sources = len(tokens)
    rows, width = tokens[0].shape
    local_experts, _, hidden = weights[0].shape
    slots = sources * CAP
    in_vmem = pl.BlockSpec(memory_space=pltpu.VMEM)
    held = [pltpu.VMEM(w.shape, w.dtype) for w in weights] if load else []
    outs = pl.pallas_call(
        functools.partial(experts_kernel, sources, local_experts, step, load),
        out_shape=[jax.ShapeDtypeStruct((rows, width), jnp.bfloat16)] * sources
        + [jax.ShapeDtypeStruct((1,), jnp.int32)]
        + held,
        in_specs=[pl.BlockSpec(memory_space=pltpu.SMEM)]
        + [in_vmem] * (sources + 1)
        + [pl.BlockSpec(memory_space=pl.ANY) if load else in_vmem] * 3,
        out_specs=[in_vmem] * sources
        + [pl.BlockSpec(memory_space=pltpu.SMEM)]
        + [in_vmem] * len(held),
        scratch_shapes=[
            pltpu.VMEM((local_experts, slots, width), jnp.bfloat16),
            pltpu.VMEM((sources, local_experts * CAP, rows), jnp.bfloat16),
            pltpu.VMEM((local_experts, slots, 1), jnp.float32),
            pltpu.VMEM((slots, hidden), jnp.bfloat16),
            pltpu.VMEM((sources, local_experts * CAP, width), jnp.bfloat16),
        ]
        + ([pltpu.SemaphoreType.DMA((local_experts, 3))] if load else []),
        compiler_params=pltpu.CompilerParams(vmem_limit_bytes=(VMEM_EXPERTS_FIRST if load else VMEM_EXPERTS) * MIB),
        cost_estimate=pl.CostEstimate(
            flops=6 * local_experts * slots * width * hidden,
            bytes_accessed=2 * (3 * local_experts * width * hidden + 2 * sources * rows * width),
            transcendentals=local_experts * slots * hidden,
        ),
        name="experts_first" if load else "experts",
    )(mark, share, *tokens, *weights)
    return list(outs[:sources]), outs[sources], list(outs[sources + 1 :]) if load else weights


def over_line(array, pairs):
    return lax.ppermute(array, "exp", [(2 * a + c, 2 * b + c) for a, b in pairs for c in (0, 1)])


def pick_kernel(mark_ref, relayed_ref, middle_ref, out_ref):
    chip = lax.div(mark_ref[0], 2)
    at_end = (chip == 0) | (chip == 3)

    @pl.when(at_end)
    def _():
        out_ref[...] = relayed_ref[...]

    @pl.when(jnp.logical_not(at_end))
    def _():
        out_ref[...] = middle_ref[...]


def take_far(far, mark, chips):
    if chips != 4:
        return lax.optimization_barrier((far, mark))[0]
    in_vmem = pl.BlockSpec(memory_space=pltpu.VMEM)
    return pl.pallas_call(
        pick_kernel,
        out_shape=jax.ShapeDtypeStruct(far[0].shape, far[0].dtype),
        in_specs=[pl.BlockSpec(memory_space=pltpu.SMEM)] + [in_vmem] * 2,
        out_specs=in_vmem,
        compiler_params=pltpu.CompilerParams(vmem_limit_bytes=4 * MIB),
        cost_estimate=pl.CostEstimate(flops=0, bytes_accessed=6 * far[0].size, transcendentals=0),
        name="pick_far",
    )(mark, *far)


def local(
    queries,
    keys,
    values,
    resid,
    out_weight,
    norm_gain,
    expert_gate,
    expert_up,
    expert_down,
    route_ids,
    route_gates,
):
    rows = queries.shape[1]
    ctx_count = lax.axis_size("ctx")
    exp_count = lax.axis_size("exp")
    chips = exp_count // 2
    ctx_me, exp_me = lax.axis_index("ctx"), lax.axis_index("exp")
    local_experts = expert_gate.shape[0]
    heads = QUERY_HEAD_COUNT // ctx_count
    group = QUERY_HEAD_COUNT // KEY_VALUE_HEADS
    kv_heads = max(1, heads // group)

    ctx_mark, exp_mark = (jnp.full((1,), me, jnp.int32) for me in (ctx_me, exp_me))
    piece = out_weight.shape[1]

    *blocks_out, pack = prepare_call(
        ctx_mark,
        queries[0],
        keys[0],
        values[0],
        out_weight,
        route_ids[0],
        route_gates[0],
        ctx_count,
        kv_heads,
        local_experts * exp_count,
    )
    blocks_in = blocks_out[:1] + [swap(blocks_out[j], "ctx", j) for j in range(1, ctx_count)]
    last = chips - 1
    pack_chips = [swap(pack, "exp", 2 * k) for k in range(1, last)]

    att = attention_call(ctx_mark, blocks_in, heads, kv_heads)
    pack_mine, pack_chips[0], att = lax.optimization_barrier((pack, pack_chips[0], att))
    if chips == 4:
        two, pack_mine, att = lax.optimization_barrier((pack_chips[1], pack_mine, att))
        pack_chips[1] = two
        middle = over_line(pack_mine, [(1, 2), (2, 1)])
        pack_far = (over_line(two, [(2, 3), (1, 0)]), middle)
    else:
        pack_far = swap(pack, "exp", 2 * last)

    def project(some):
        mine = projection_call(att, some, ctx_count)
        return [mine[0]] + [swap(mine[j], "ctx", j) for j in range(1, ctx_count)]

    def with_pair(arrays):
        return [both for a in arrays for both in (a, swap(a, "exp", 1))]

    packs = with_pair([pack_mine, pack_chips[0]])
    parts = project(packs)
    packs_middle = with_pair(pack_chips[1:])
    parts_middle = project(packs_middle)
    pack_far, parts, parts_middle[0] = lax.optimization_barrier((pack_far, parts, parts_middle[0]))
    packs_last = with_pair([take_far(pack_far, exp_mark, chips)])
    parts = parts + parts_middle + project(packs_last)
    share = jnp.stack([p[out_weight.shape[0] :] for p in packs + packs_middle + packs_last])
    parts[0], share = lax.optimization_barrier((parts[0], share))
    attn_resid, normed = norm_call(exp_mark, resid[0], norm_gain, parts, ctx_count, piece)

    def experts(which, mark, tokens, weights):
        at = slice(2 * which.start, 2 * which.stop)
        return experts_call(mark, share[at], with_pair(tokens), weights, which.start == 0)

    def pair_sum(both):
        return both[0].astype(jnp.float32) + swap(both[1], "exp", 1).astype(jnp.float32)

    near = [swap(normed, "exp", 2 * k) for k in range(1, last)]
    partial, mark, weights = experts(
        slice(0, 1), exp_mark, [normed], [expert_gate, expert_up, expert_down]
    )
    if chips == 4:
        near[1], normed, mark = lax.optimization_barrier((near[1], normed, mark))
        far = (
            over_line(near[1], [(2, 3), (1, 0)]),
            over_line(normed, [(1, 2), (2, 1)]),
        )
    else:
        far = swap(normed, "exp", 2 * last)
    layer_out = attn_resid.astype(jnp.float32) + pair_sum(partial)
    partial, mark, _ = experts(slice(1, last), mark, near, weights)
    sums = [pair_sum(partial[2 * k :]).astype(jnp.bfloat16) for k in range(last - 1)]
    partial, _, _ = experts(slice(last, chips), mark, [take_far(far, mark, chips)], weights)
    sum_far = pair_sum(partial).astype(jnp.bfloat16)
    if chips == 4:
        relayed = over_line(sum_far, [(3, 2), (0, 1)])
        terms = [swap(sums[0], "exp", 2), over_line(sum_far, [(1, 2), (2, 1)])]
        both = sums[1].astype(jnp.float32) + relayed.astype(jnp.float32)
        final = swap(both.astype(jnp.bfloat16), "exp", 4)
    else:
        terms = [swap(p, "exp", 2 * k) for k, p in enumerate(sums, 1)]
        final = swap(sum_far, "exp", 2 * last)
    for s in terms:
        layer_out = layer_out + s.astype(jnp.float32)
    layer_out = lax.optimization_barrier(layer_out) + final.astype(jnp.float32)
    return (attn_resid[None], layer_out.astype(jnp.bfloat16)[None])


def solution(mesh):
    in_specs = (
        P("exp", "ctx", None),
        P("exp", "ctx", None),
        P("exp", "ctx", None),
        P("exp", "ctx", None),
        P("ctx", "exp"),
        P(),
        P("exp", None, None),
        P("exp", None, None),
        P("exp", None, None),
        P("exp", "ctx", None),
        P("exp", "ctx", None),
    )
    out_specs = (P("exp", "ctx", None), P("exp", "ctx", None))
    return jax.shard_map(local, mesh=mesh, in_specs=in_specs, out_specs=out_specs, check_vma=False)
```

```python
import functools
import math

import jax
import jax.numpy as jnp
from jax import lax
from jax.experimental import pallas as pl
from jax.experimental.pallas import tpu as pltpu
from jax.sharding import PartitionSpec as P

QUERY_HEAD_COUNT = 32
KEY_VALUE_HEADS = 4
HEAD_SIZE = 128
TOPK = 8
CAP = 64

norm_eps = 1e-06
mask_fill_value = -1e30
MIB = 1024 * 1024
VMEM_EXPERTS = 14
VMEM_EXPERTS_FIRST = 32
VMEM_PREPARE = 58


def swap(shard, axis, by):
    devices = lax.axis_size(axis)
    return lax.ppermute(shard, axis, [(i, i ^ by) for i in range(devices)])


def dot(a, b):
    return jnp.dot(a, b, preferred_element_type=jnp.float32)


def prepare_kernel(blocks, kv_heads, experts, marks_ref, q_ref, k_ref, v_ref, w_ref, ids_ref, gates_ref, *refs):
    outs, pack_ref, sems = refs[:blocks], refs[blocks], refs[blocks + 1]
    rows, width = q_ref.shape
    depth, piece = w_ref.shape
    wide, kv_wide = width // blocks, kv_heads * HEAD_SIZE
    group = QUERY_HEAD_COUNT // KEY_VALUE_HEADS
    copies = []
    for j in list(range(1, blocks)) + [0]:
        who = marks_ref[0] ^ j
        at = pl.ds(pl.multiple_of(who * wide, HEAD_SIZE), wide)
        kv_at = lax.div(who * (wide // HEAD_SIZE), group) * HEAD_SIZE
        kv_at = pl.ds(pl.multiple_of(kv_at, HEAD_SIZE), kv_wide)
        copies += [
            pltpu.make_async_copy(q_ref.at[:, at], outs[j].at[:, :wide], sems.at[3 * j]),
            pltpu.make_async_copy(
                k_ref.at[:, kv_at], outs[j].at[:, wide : wide + kv_wide], sems.at[3 * j + 1]
            ),
            pltpu.make_async_copy(
                v_ref.at[:, kv_at], outs[j].at[:, wide + kv_wide :], sems.at[3 * j + 2]
            ),
        ]
    copies.append(pltpu.make_async_copy(w_ref, pack_ref.at[:depth, :], sems.at[3 * blocks]))
    for copy in copies:
        copy.start()
    gates = gates_ref[...]
    shares = gates / jnp.sum(gates, axis=0, keepdims=True)
    expert = lax.broadcasted_iota(jnp.int32, (experts, rows), 0)
    by_expert = jnp.zeros((experts, rows), jnp.float32)
    for n in range(TOPK):
        by_expert += jnp.where(ids_ref[n : n + 1, :] == expert, shares[n : n + 1, :], 0.0)
    high = by_expert.astype(jnp.bfloat16)
    low = (by_expert - high.astype(jnp.float32)).astype(jnp.bfloat16)
    if piece >= 2 * rows:
        pack_ref[depth:, :rows] = high
        pack_ref[depth:, rows : 2 * rows] = low
    else:
        pack_ref[depth : depth + experts, :rows] = high
        pack_ref[depth + experts :, :rows] = low
    for copy in copies:
        copy.wait()


def prepare_call(marks, q, k, v, w, ids, gates, blocks, kv_heads, experts):
    rows, width = q.shape
    depth, piece = w.shape
    extra = experts if piece >= 2 * rows else 2 * experts
    wide = width // blocks + 2 * kv_heads * HEAD_SIZE
    in_vmem = pl.BlockSpec(memory_space=pltpu.VMEM)
    return pl.pallas_call(
        functools.partial(prepare_kernel, blocks, kv_heads, experts),
        out_shape=[pltpu.VMEM((rows, wide), jnp.bfloat16)] * blocks
        + [pltpu.VMEM((depth + extra, piece), jnp.bfloat16)],
        in_specs=[pl.BlockSpec(memory_space=pltpu.SMEM)]
        + [pl.BlockSpec(memory_space=pltpu.HBM)] * 4
        + [in_vmem] * 2,
        out_specs=[in_vmem] * (blocks + 1),
        scratch_shapes=[pltpu.SemaphoreType.DMA((3 * blocks + 1,))],
        compiler_params=pltpu.CompilerParams(vmem_limit_bytes=VMEM_PREPARE * MIB),
        cost_estimate=pl.CostEstimate(
            flops=rows * experts * 4 * TOPK,
            bytes_accessed=4 * (rows * (width + 4 * kv_heads * HEAD_SIZE) + depth * piece),
            transcendentals=0,
        ),
        name="prepare",
    )(marks, q, k, v, w, ids.T, gates.T)


STACK = 4


def attention_kernel(blocks, heads, kv_heads, me_ref, *refs):
    ins, out_ref = refs[:blocks], refs[blocks]
    query_rows, key_rows, value_rows = refs[blocks + 1 :]
    rows = ins[0].shape[0]
    me = me_ref[0]
    wide = heads * HEAD_SIZE
    value_rows[:, :, HEAD_SIZE:] = jnp.ones(value_rows.shape[:2] + (HEAD_SIZE,), jnp.bfloat16)
    for j in range(blocks):
        at = pl.ds(pl.multiple_of((me ^ j) * rows, rows), rows)
        for h in range(heads):
            query_rows[h, at, :] = ins[j][:, h * HEAD_SIZE : (h + 1) * HEAD_SIZE]
        for g in range(kv_heads):
            key_at, value_at = wide + g * HEAD_SIZE, wide + (kv_heads + g) * HEAD_SIZE
            key_rows[g, at, :] = ins[j][:, key_at : key_at + HEAD_SIZE]
            value_rows[g, at, :HEAD_SIZE] = ins[j][:, value_at : value_at + HEAD_SIZE]
    group = heads // kv_heads
    stack = min(STACK, group)
    row = lax.broadcasted_iota(jnp.int32, (rows, rows), 0)
    col = lax.broadcasted_iota(jnp.int32, (rows, rows), 1)
    allowed = jnp.concatenate([row >= col] * stack, axis=0)
    factor = HEAD_SIZE ** (-0.5) * math.log2(math.e)
    for h in range(0, heads, stack):
        g = h // group
        for i in range(blocks):
            q = query_rows[h : h + stack, i * rows : (i + 1) * rows, :]
            s = lax.dot_general(
                q.reshape(stack * rows, HEAD_SIZE),
                key_rows[g, : (i + 1) * rows, :],
                (((1,), (1,)), ((), ())),
                preferred_element_type=jnp.float32,
            )
            last = jnp.where(allowed, s[:, i * rows :], mask_fill_value)
            s = last if i == 0 else jnp.concatenate([s[:, : i * rows], last], axis=1)
            p = jnp.exp2((s - jnp.max(s, axis=1, keepdims=True)) * factor)
            o = dot(p.astype(jnp.bfloat16), value_rows[g, : (i + 1) * rows, :])
            o = (o[:, :HEAD_SIZE] / o[:, HEAD_SIZE:]).astype(jnp.bfloat16)
            at = pl.ds(pl.multiple_of((me ^ i) * rows, rows), rows)
            for n in range(stack):
                out_ref[at, (h + n) * HEAD_SIZE : (h + n + 1) * HEAD_SIZE] = o[
                    n * rows : (n + 1) * rows
                ]


def attention_call(me, ins, heads, kv_heads):
    blocks = len(ins)
    rows, wide_in = ins[0].shape
    length, wide = blocks * rows, heads * HEAD_SIZE
    return pl.pallas_call(
        functools.partial(attention_kernel, blocks, heads, kv_heads),
        out_shape=jax.ShapeDtypeStruct((length, wide), jnp.bfloat16),
        in_specs=[pl.BlockSpec(memory_space=pltpu.SMEM)]
        + [pl.BlockSpec(memory_space=pltpu.VMEM)] * blocks,
        out_specs=pl.BlockSpec(memory_space=pltpu.VMEM),
        scratch_shapes=[
            pltpu.VMEM((heads, length, HEAD_SIZE), jnp.bfloat16),
            pltpu.VMEM((kv_heads, length, HEAD_SIZE), jnp.bfloat16),
            pltpu.VMEM((kv_heads, length, 2 * HEAD_SIZE), jnp.bfloat16),
        ],
        compiler_params=pltpu.CompilerParams(vmem_limit_bytes=24 * MIB),
        cost_estimate=pl.CostEstimate(
            flops=4 * length * length * wide,
            bytes_accessed=4 * length * wide_in,
            transcendentals=length * length * heads,
        ),
        name="attention",
    )(me, *ins)


def projection_kernel(pieces, att_ref, *refs):
    ins, outs = refs[:pieces], refs[pieces:]
    rows = outs[0].shape[0]
    depth = att_ref.shape[1]
    piece = ins[0].shape[1]
    for k in range(pieces):
        y = dot(att_ref[...], ins[k][:depth, :]).astype(jnp.bfloat16)
        for j, out in enumerate(outs):
            out[:, k * piece : (k + 1) * piece] = y[j * rows : (j + 1) * rows]


def projection_call(att, packs, blocks):
    length, depth = att.shape
    piece = packs[0].shape[1]
    rows, wide = length // blocks, piece * len(packs)
    return pl.pallas_call(
        functools.partial(projection_kernel, len(packs)),
        out_shape=[jax.ShapeDtypeStruct((rows, wide), jnp.bfloat16)] * blocks,
        in_specs=[pl.BlockSpec(memory_space=pltpu.VMEM)] * (1 + len(packs)),
        out_specs=[pl.BlockSpec(memory_space=pltpu.VMEM)] * blocks,
        compiler_params=pltpu.CompilerParams(vmem_limit_bytes=8 * MIB),
        cost_estimate=pl.CostEstimate(
            flops=2 * length * depth * wide,
            bytes_accessed=2 * (length * depth + depth * wide + length * wide),
            transcendentals=0,
        ),
        name="projection",
    )(att, *packs)


def norm_kernel(chunks, blocks, piece, me_ref, resid_ref, gain_ref, *refs):
    parts, (attn_ref, normed_ref) = refs[: chunks * blocks], refs[chunks * blocks :]
    me = me_ref[0]
    width = resid_ref.shape[1]
    total = None
    order = 0
    for n in range(chunks):
        for k in range(parts[n * blocks].shape[1] // piece):
            at = pl.ds(pl.multiple_of((me ^ order) * piece, piece), piece)
            order += 1
            acc = resid_ref[:, at].astype(jnp.float32)
            for j in range(blocks):
                acc = acc + parts[n * blocks + j][:, k * piece : (k + 1) * piece].astype(
                    jnp.float32
                )
            acc = acc.astype(jnp.bfloat16)
            attn_ref[:, at] = acc
            acc = acc.astype(jnp.float32)
            squares = jnp.sum(acc * acc, axis=1, keepdims=True)
            total = squares if total is None else total + squares
    scale = lax.rsqrt(total / width + norm_eps)
    normed_ref[...] = (attn_ref[...].astype(jnp.float32) * scale * gain_ref[...]).astype(
        jnp.bfloat16
    )


def norm_call(me, resid, gain, parts, blocks, piece):
    rows, width = resid.shape
    return pl.pallas_call(
        functools.partial(norm_kernel, len(parts) // blocks, blocks, piece),
        out_shape=[jax.ShapeDtypeStruct((rows, width), jnp.bfloat16)] * 2,
        in_specs=[pl.BlockSpec(memory_space=pltpu.SMEM)]
        + [pl.BlockSpec(memory_space=pltpu.VMEM)] * (2 + len(parts)),
        out_specs=[pl.BlockSpec(memory_space=pltpu.VMEM)] * 2,
        compiler_params=pltpu.CompilerParams(vmem_limit_bytes=8 * MIB),
        cost_estimate=pl.CostEstimate(
            flops=10 * rows * width, bytes_accessed=2 * rows * width * 8, transcendentals=rows
        ),
        name="resid_norm",
    )(me, resid, gain.reshape(1, width), *parts)


def experts_kernel(sources, local_experts, step, load, mark_ref, share_ref, *refs):
    ins = refs[:sources]
    weights = refs[sources : sources + 3]
    outs = refs[sources + 3 : 2 * sources + 3]
    refs[2 * sources + 3][0] = mark_ref[0]
    refs = refs[2 * sources + 4 :]
    copies = [[] for _ in range(local_experts)]
    if load:
        held, refs, sems = refs[:3], refs[3:-1], refs[-1]
        for n in range(local_experts):
            for m in range(3):
                copy = pltpu.make_async_copy(weights[m].at[n], held[m].at[n], sems.at[n, m])
                copy.start()
                copies[n].append(copy)
        weights = held
    gate_ref, up_ref, down_ref = weights
    picked, slot_map, slot_share, hidden_rows, slot_out = refs
    rows = ins[0].shape[0]
    _, width, hidden = gate_ref.shape
    before = (
        lax.broadcasted_iota(jnp.int32, (rows, rows), 0)
        < lax.broadcasted_iota(jnp.int32, (rows, rows), 1)
    ).astype(jnp.bfloat16)
    slot = lax.broadcasted_iota(jnp.int32, (CAP, rows), 0).astype(jnp.float32)
    for s in range(sources):
        both = share_ref[s].astype(jnp.float32)
        if both.shape[1] >= 2 * rows:
            both = both[:, :rows] + both[:, rows : 2 * rows]
        else:
            both = both[: both.shape[0] // 2, :rows] + both[both.shape[0] // 2 :, :rows]
        expert = lax.broadcasted_iota(jnp.int32, both.shape, 0)
        place = lax.broadcasted_iota(jnp.int32, (8, rows), 0)
        share = jnp.zeros((8, rows), jnp.float32)
        for n in range(local_experts):
            mine = jnp.where(expert == mark_ref[0] * local_experts + n, both, 0.0)
            share = jnp.where(place == n, jnp.sum(mine, axis=0, keepdims=True), share)
        rank = dot((share > 0.0).astype(jnp.bfloat16), before)
        rank = jnp.where(share > 0.0, rank, -1.0)
        for n in range(local_experts):
            taken = slot == rank[n : n + 1, :]
            slot_map[s, n * CAP : (n + 1) * CAP, :] = taken.astype(jnp.bfloat16)
            slot_share[n, s * CAP : (s + 1) * CAP, :] = jnp.sum(
                jnp.where(taken, share[n : n + 1, :], 0.0), axis=1, keepdims=True
            )
        rows_picked = dot(slot_map[s], ins[s][...]).astype(jnp.bfloat16)
        for n in range(local_experts):
            picked[n, s * CAP : (s + 1) * CAP, :] = rows_picked[n * CAP : (n + 1) * CAP]
    for n in range(local_experts):
        for copy in copies[n]:
            copy.wait()
        x = picked[n]
        for at in range(0, hidden, step):
            gate_part = dot(x, gate_ref[n, :, at : at + step])
            up_part = dot(x, up_ref[n, :, at : at + step])
            activated = gate_part / (1.0 + jnp.exp(-gate_part)) * up_part * slot_share[n]
            hidden_rows[:, at : at + step] = activated.astype(jnp.bfloat16)
        for at in range(0, width, 2 * step):
            y = dot(hidden_rows[...], down_ref[n, :, at : at + 2 * step]).astype(jnp.bfloat16)
            for s in range(sources):
                slot_out[s, n * CAP : (n + 1) * CAP, at : at + 2 * step] = y[
                    s * CAP : (s + 1) * CAP
                ]
    for s in range(sources):
        outs[s][...] = lax.dot_general(
            slot_map[s], slot_out[s], (((0,), (0,)), ((), ())), preferred_element_type=jnp.float32
        ).astype(jnp.bfloat16)


def experts_call(mark, share, tokens, weights, load, step=256):
    sources = len(tokens)
    rows, width = tokens[0].shape
    local_experts, _, hidden = weights[0].shape
    slots = sources * CAP
    in_vmem = pl.BlockSpec(memory_space=pltpu.VMEM)
    held = [pltpu.VMEM(w.shape, w.dtype) for w in weights] if load else []
    outs = pl.pallas_call(
        functools.partial(experts_kernel, sources, local_experts, step, load),
        out_shape=[jax.ShapeDtypeStruct((rows, width), jnp.bfloat16)] * sources
        + [jax.ShapeDtypeStruct((1,), jnp.int32)]
        + held,
        in_specs=[pl.BlockSpec(memory_space=pltpu.SMEM)]
        + [in_vmem] * (sources + 1)
        + [pl.BlockSpec(memory_space=pl.ANY) if load else in_vmem] * 3,
        out_specs=[in_vmem] * sources
        + [pl.BlockSpec(memory_space=pltpu.SMEM)]
        + [in_vmem] * len(held),
        scratch_shapes=[
            pltpu.VMEM((local_experts, slots, width), jnp.bfloat16),
            pltpu.VMEM((sources, local_experts * CAP, rows), jnp.bfloat16),
            pltpu.VMEM((local_experts, slots, 1), jnp.float32),
            pltpu.VMEM((slots, hidden), jnp.bfloat16),
            pltpu.VMEM((sources, local_experts * CAP, width), jnp.bfloat16),
        ]
        + ([pltpu.SemaphoreType.DMA((local_experts, 3))] if load else []),
        compiler_params=pltpu.CompilerParams(vmem_limit_bytes=(VMEM_EXPERTS_FIRST if load else VMEM_EXPERTS) * MIB),
        cost_estimate=pl.CostEstimate(
            flops=6 * local_experts * slots * width * hidden,
            bytes_accessed=2 * (3 * local_experts * width * hidden + 2 * sources * rows * width),
            transcendentals=local_experts * slots * hidden,
        ),
        name="experts_first" if load else "experts",
    )(mark, share, *tokens, *weights)
    return list(outs[:sources]), outs[sources], list(outs[sources + 1 :]) if load else weights


def over_line(array, pairs):
    return lax.ppermute(array, "exp", [(2 * a + c, 2 * b + c) for a, b in pairs for c in (0, 1)])


def pick_kernel(mark_ref, relayed_ref, middle_ref, out_ref):
    chip = lax.div(mark_ref[0], 2)
    at_end = (chip == 0) | (chip == 3)

    @pl.when(at_end)
    def _():
        out_ref[...] = relayed_ref[...]

    @pl.when(jnp.logical_not(at_end))
    def _():
        out_ref[...] = middle_ref[...]


def take_far(far, mark, chips):
    if chips != 4:
        return lax.optimization_barrier((far, mark))[0]
    in_vmem = pl.BlockSpec(memory_space=pltpu.VMEM)
    return pl.pallas_call(
        pick_kernel,
        out_shape=jax.ShapeDtypeStruct(far[0].shape, far[0].dtype),
        in_specs=[pl.BlockSpec(memory_space=pltpu.SMEM)] + [in_vmem] * 2,
        out_specs=in_vmem,
        compiler_params=pltpu.CompilerParams(vmem_limit_bytes=4 * MIB),
        cost_estimate=pl.CostEstimate(flops=0, bytes_accessed=6 * far[0].size, transcendentals=0),
        name="pick_far",
    )(mark, *far)


def local(
    queries,
    keys,
    values,
    resid,
    out_weight,
    norm_gain,
    expert_gate,
    expert_up,
    expert_down,
    route_ids,
    route_gates,
):
    rows = queries.shape[1]
    ctx_count = lax.axis_size("ctx")
    exp_count = lax.axis_size("exp")
    chips = exp_count // 2
    ctx_me, exp_me = lax.axis_index("ctx"), lax.axis_index("exp")
    local_experts = expert_gate.shape[0]
    heads = QUERY_HEAD_COUNT // ctx_count
    group = QUERY_HEAD_COUNT // KEY_VALUE_HEADS
    kv_heads = max(1, heads // group)

    ctx_mark, exp_mark = (jnp.full((1,), me, jnp.int32) for me in (ctx_me, exp_me))
    piece = out_weight.shape[1]

    *blocks_out, pack = prepare_call(
        ctx_mark,
        queries[0],
        keys[0],
        values[0],
        out_weight,
        route_ids[0],
        route_gates[0],
        ctx_count,
        kv_heads,
        local_experts * exp_count,
    )
    blocks_in = blocks_out[:1] + [swap(blocks_out[j], "ctx", j) for j in range(1, ctx_count)]
    last = chips - 1
    pack_chips = [swap(pack, "exp", 2 * k) for k in range(1, last)]

    att = attention_call(ctx_mark, blocks_in, heads, kv_heads)
    pack_mine, pack_chips[0], att = lax.optimization_barrier((pack, pack_chips[0], att))
    if chips == 4:
        two, pack_mine, att = lax.optimization_barrier((pack_chips[1], pack_mine, att))
        pack_chips[1] = two
        middle = over_line(pack_mine, [(1, 2), (2, 1)])
        pack_far = (over_line(two, [(2, 3), (1, 0)]), middle)
    else:
        pack_far = swap(pack, "exp", 2 * last)

    def project(some):
        mine = projection_call(att, some, ctx_count)
        return [mine[0]] + [swap(mine[j], "ctx", j) for j in range(1, ctx_count)]

    def with_pair(arrays):
        return [both for a in arrays for both in (a, swap(a, "exp", 1))]

    packs = with_pair([pack_mine, pack_chips[0]])
    parts = project(packs)
    packs_middle = with_pair(pack_chips[1:])
    parts_middle = project(packs_middle)
    pack_far, parts, parts_middle[0] = lax.optimization_barrier((pack_far, parts, parts_middle[0]))
    packs_last = with_pair([take_far(pack_far, exp_mark, chips)])
    parts = parts + parts_middle + project(packs_last)
    share = jnp.stack([p[out_weight.shape[0] :] for p in packs + packs_middle + packs_last])
    parts[0], share = lax.optimization_barrier((parts[0], share))
    attn_resid, normed = norm_call(exp_mark, resid[0], norm_gain, parts, ctx_count, piece)

    def experts(which, mark, tokens, weights):
        at = slice(2 * which.start, 2 * which.stop)
        return experts_call(mark, share[at], with_pair(tokens), weights, which.start == 0)

    def pair_sum(both):
        return both[0].astype(jnp.float32) + swap(both[1], "exp", 1).astype(jnp.float32)

    near = [swap(normed, "exp", 2 * k) for k in range(1, last)]
    partial, mark, weights = experts(
        slice(0, 1), exp_mark, [normed], [expert_gate, expert_up, expert_down]
    )
    if chips == 4:
        near[1], normed, mark = lax.optimization_barrier((near[1], normed, mark))
        far = (
            over_line(near[1], [(2, 3), (1, 0)]),
            over_line(normed, [(1, 2), (2, 1)]),
        )
    else:
        far = swap(normed, "exp", 2 * last)
    layer_out = attn_resid.astype(jnp.float32) + pair_sum(partial)
    partial, mark, _ = experts(slice(1, last), mark, near, weights)
    sums = [pair_sum(partial[2 * k :]).astype(jnp.bfloat16) for k in range(last - 1)]
    partial, _, _ = experts(slice(last, chips), mark, [take_far(far, mark, chips)], weights)
    sum_far = pair_sum(partial).astype(jnp.bfloat16)
    if chips == 4:
        def add(a, b):
            return (a.astype(jnp.float32) + b.astype(jnp.float32)).astype(jnp.bfloat16)

        relayed = over_line(sum_far, [(3, 2), (0, 1)])
        early = over_line(sums[1], [(0, 1), (3, 2)])
        middle = over_line(add(sum_far, early), [(1, 2), (2, 1)])
        both, middle = lax.optimization_barrier((add(sums[1], relayed), middle))
        terms = [swap(sums[0], "exp", 2), middle]
        final = over_line(both, [(2, 0), (1, 3)])
    else:
        terms = [swap(p, "exp", 2 * k) for k, p in enumerate(sums, 1)]
        final = swap(sum_far, "exp", 2 * last)
    for s in terms:
        layer_out = layer_out + s.astype(jnp.float32)
    layer_out = lax.optimization_barrier(layer_out) + final.astype(jnp.float32)
    return (attn_resid[None], layer_out.astype(jnp.bfloat16)[None])


def solution(mesh):
    in_specs = (
        P("exp", "ctx", None),
        P("exp", "ctx", None),
        P("exp", "ctx", None),
        P("exp", "ctx", None),
        P("ctx", "exp"),
        P(),
        P("exp", None, None),
        P("exp", None, None),
        P("exp", None, None),
        P("exp", "ctx", None),
        P("exp", "ctx", None),
    )
    out_specs = (P("exp", "ctx", None), P("exp", "ctx", None))
    return jax.shard_map(local, mesh=mesh, in_specs=in_specs, out_specs=out_specs, check_vma=False)
```

```python
import functools
import math

import jax
import jax.numpy as jnp
from jax import lax
from jax.experimental import pallas as pl
from jax.experimental.pallas import tpu as pltpu
from jax.sharding import PartitionSpec as P

QUERY_HEAD_COUNT = 32
KEY_VALUE_HEADS = 4
HEAD_SIZE = 128
TOPK = 8
CAP = 64

norm_eps = 1e-06
mask_fill_value = -1e30
MIB = 1024 * 1024
VMEM_EXPERTS = 14
VMEM_EXPERTS_FIRST = 32
VMEM_PREPARE = 58


def swap(shard, axis, by):
    devices = lax.axis_size(axis)
    return lax.ppermute(shard, axis, [(i, i ^ by) for i in range(devices)])


def dot(a, b):
    return jnp.dot(a, b, preferred_element_type=jnp.float32)


def prepare_kernel(blocks, kv_heads, experts, marks_ref, q_ref, k_ref, v_ref, w_ref, ids_ref, gates_ref, *refs):
    outs, pack_ref, sems = refs[:blocks], refs[blocks], refs[blocks + 1]
    rows, width = q_ref.shape
    depth, piece = w_ref.shape
    wide, kv_wide = width // blocks, kv_heads * HEAD_SIZE
    group = QUERY_HEAD_COUNT // KEY_VALUE_HEADS
    copies = []
    for j in list(range(1, blocks)) + [0]:
        who = marks_ref[0] ^ j
        at = pl.ds(pl.multiple_of(who * wide, HEAD_SIZE), wide)
        kv_at = lax.div(who * (wide // HEAD_SIZE), group) * HEAD_SIZE
        kv_at = pl.ds(pl.multiple_of(kv_at, HEAD_SIZE), kv_wide)
        copies += [
            pltpu.make_async_copy(q_ref.at[:, at], outs[j].at[:, :wide], sems.at[3 * j]),
            pltpu.make_async_copy(
                k_ref.at[:, kv_at], outs[j].at[:, wide : wide + kv_wide], sems.at[3 * j + 1]
            ),
            pltpu.make_async_copy(
                v_ref.at[:, kv_at], outs[j].at[:, wide + kv_wide :], sems.at[3 * j + 2]
            ),
        ]
    copies.append(pltpu.make_async_copy(w_ref, pack_ref.at[:depth, :], sems.at[3 * blocks]))
    for copy in copies:
        copy.start()
    gates = gates_ref[...]
    shares = gates / jnp.sum(gates, axis=0, keepdims=True)
    expert = lax.broadcasted_iota(jnp.int32, (experts, rows), 0)
    by_expert = jnp.zeros((experts, rows), jnp.float32)
    for n in range(TOPK):
        by_expert += jnp.where(ids_ref[n : n + 1, :] == expert, shares[n : n + 1, :], 0.0)
    high = by_expert.astype(jnp.bfloat16)
    low = (by_expert - high.astype(jnp.float32)).astype(jnp.bfloat16)
    if piece >= 2 * rows:
        pack_ref[depth:, :rows] = high
        pack_ref[depth:, rows : 2 * rows] = low
    else:
        pack_ref[depth : depth + experts, :rows] = high
        pack_ref[depth + experts :, :rows] = low
    for copy in copies:
        copy.wait()


def prepare_call(marks, q, k, v, w, ids, gates, blocks, kv_heads, experts):
    rows, width = q.shape
    depth, piece = w.shape
    extra = experts if piece >= 2 * rows else 2 * experts
    wide = width // blocks + 2 * kv_heads * HEAD_SIZE
    in_vmem = pl.BlockSpec(memory_space=pltpu.VMEM)
    return pl.pallas_call(
        functools.partial(prepare_kernel, blocks, kv_heads, experts),
        out_shape=[pltpu.VMEM((rows, wide), jnp.bfloat16)] * blocks
        + [pltpu.VMEM((depth + extra, piece), jnp.bfloat16)],
        in_specs=[pl.BlockSpec(memory_space=pltpu.SMEM)]
        + [pl.BlockSpec(memory_space=pltpu.HBM)] * 4
        + [in_vmem] * 2,
        out_specs=[in_vmem] * (blocks + 1),
        scratch_shapes=[pltpu.SemaphoreType.DMA((3 * blocks + 1,))],
        compiler_params=pltpu.CompilerParams(vmem_limit_bytes=VMEM_PREPARE * MIB),
        cost_estimate=pl.CostEstimate(
            flops=rows * experts * 4 * TOPK,
            bytes_accessed=4 * (rows * (width + 4 * kv_heads * HEAD_SIZE) + depth * piece),
            transcendentals=0,
        ),
        name="prepare",
    )(marks, q, k, v, w, ids.T, gates.T)


STACK = 4


def attention_kernel(blocks, heads, kv_heads, me_ref, *refs):
    ins, out_ref = refs[:blocks], refs[blocks]
    query_rows, key_rows, value_rows = refs[blocks + 1 :]
    rows = ins[0].shape[0]
    me = me_ref[0]
    wide = heads * HEAD_SIZE
    value_rows[:, :, HEAD_SIZE:] = jnp.ones(value_rows.shape[:2] + (HEAD_SIZE,), jnp.bfloat16)
    for j in range(blocks):
        at = pl.ds(pl.multiple_of((me ^ j) * rows, rows), rows)
        for h in range(heads):
            query_rows[h, at, :] = ins[j][:, h * HEAD_SIZE : (h + 1) * HEAD_SIZE]
        for g in range(kv_heads):
            key_at, value_at = wide + g * HEAD_SIZE, wide + (kv_heads + g) * HEAD_SIZE
            key_rows[g, at, :] = ins[j][:, key_at : key_at + HEAD_SIZE]
            value_rows[g, at, :HEAD_SIZE] = ins[j][:, value_at : value_at + HEAD_SIZE]
    group = heads // kv_heads
    stack = min(STACK, group)
    row = lax.broadcasted_iota(jnp.int32, (rows, rows), 0)
    col = lax.broadcasted_iota(jnp.int32, (rows, rows), 1)
    allowed = jnp.concatenate([row >= col] * stack, axis=0)
    factor = HEAD_SIZE ** (-0.5) * math.log2(math.e)
    for h in range(0, heads, stack):
        g = h // group
        for i in range(blocks):
            q = query_rows[h : h + stack, i * rows : (i + 1) * rows, :]
            s = lax.dot_general(
                q.reshape(stack * rows, HEAD_SIZE),
                key_rows[g, : (i + 1) * rows, :],
                (((1,), (1,)), ((), ())),
                preferred_element_type=jnp.float32,
            )
            last = jnp.where(allowed, s[:, i * rows :], mask_fill_value)
            s = last if i == 0 else jnp.concatenate([s[:, : i * rows], last], axis=1)
            p = jnp.exp2((s - jnp.max(s, axis=1, keepdims=True)) * factor)
            o = dot(p.astype(jnp.bfloat16), value_rows[g, : (i + 1) * rows, :])
            o = (o[:, :HEAD_SIZE] / o[:, HEAD_SIZE:]).astype(jnp.bfloat16)
            at = pl.ds(pl.multiple_of((me ^ i) * rows, rows), rows)
            for n in range(stack):
                out_ref[at, (h + n) * HEAD_SIZE : (h + n + 1) * HEAD_SIZE] = o[
                    n * rows : (n + 1) * rows
                ]


def attention_call(me, ins, heads, kv_heads):
    blocks = len(ins)
    rows, wide_in = ins[0].shape
    length, wide = blocks * rows, heads * HEAD_SIZE
    return pl.pallas_call(
        functools.partial(attention_kernel, blocks, heads, kv_heads),
        out_shape=jax.ShapeDtypeStruct((length, wide), jnp.bfloat16),
        in_specs=[pl.BlockSpec(memory_space=pltpu.SMEM)]
        + [pl.BlockSpec(memory_space=pltpu.VMEM)] * blocks,
        out_specs=pl.BlockSpec(memory_space=pltpu.VMEM),
        scratch_shapes=[
            pltpu.VMEM((heads, length, HEAD_SIZE), jnp.bfloat16),
            pltpu.VMEM((kv_heads, length, HEAD_SIZE), jnp.bfloat16),
            pltpu.VMEM((kv_heads, length, 2 * HEAD_SIZE), jnp.bfloat16),
        ],
        compiler_params=pltpu.CompilerParams(vmem_limit_bytes=24 * MIB),
        cost_estimate=pl.CostEstimate(
            flops=4 * length * length * wide,
            bytes_accessed=4 * length * wide_in,
            transcendentals=length * length * heads,
        ),
        name="attention",
    )(me, *ins)


def projection_kernel(pieces, att_ref, *refs):
    ins, outs = refs[:pieces], refs[pieces:]
    rows = outs[0].shape[0]
    depth = att_ref.shape[1]
    piece = ins[0].shape[1]
    for k in range(pieces):
        y = dot(att_ref[...], ins[k][:depth, :]).astype(jnp.bfloat16)
        for j, out in enumerate(outs):
            out[:, k * piece : (k + 1) * piece] = y[j * rows : (j + 1) * rows]


def projection_call(att, packs, blocks):
    length, depth = att.shape
    piece = packs[0].shape[1]
    rows, wide = length // blocks, piece * len(packs)
    return pl.pallas_call(
        functools.partial(projection_kernel, len(packs)),
        out_shape=[jax.ShapeDtypeStruct((rows, wide), jnp.bfloat16)] * blocks,
        in_specs=[pl.BlockSpec(memory_space=pltpu.VMEM)] * (1 + len(packs)),
        out_specs=[pl.BlockSpec(memory_space=pltpu.VMEM)] * blocks,
        compiler_params=pltpu.CompilerParams(vmem_limit_bytes=8 * MIB),
        cost_estimate=pl.CostEstimate(
            flops=2 * length * depth * wide,
            bytes_accessed=2 * (length * depth + depth * wide + length * wide),
            transcendentals=0,
        ),
        name="projection",
    )(att, *packs)


def norm_kernel(chunks, blocks, piece, me_ref, resid_ref, gain_ref, *refs):
    parts, (attn_ref, normed_ref) = refs[: chunks * blocks], refs[chunks * blocks :]
    me = me_ref[0]
    width = resid_ref.shape[1]
    total = None
    order = 0
    for n in range(chunks):
        for k in range(parts[n * blocks].shape[1] // piece):
            at = pl.ds(pl.multiple_of((me ^ order) * piece, piece), piece)
            order += 1
            acc = resid_ref[:, at].astype(jnp.float32)
            for j in range(blocks):
                acc = acc + parts[n * blocks + j][:, k * piece : (k + 1) * piece].astype(
                    jnp.float32
                )
            acc = acc.astype(jnp.bfloat16)
            attn_ref[:, at] = acc
            acc = acc.astype(jnp.float32)
            squares = jnp.sum(acc * acc, axis=1, keepdims=True)
            total = squares if total is None else total + squares
    scale = lax.rsqrt(total / width + norm_eps)
    normed_ref[...] = (attn_ref[...].astype(jnp.float32) * scale * gain_ref[...]).astype(
        jnp.bfloat16
    )


def norm_call(me, resid, gain, parts, blocks, piece):
    rows, width = resid.shape
    return pl.pallas_call(
        functools.partial(norm_kernel, len(parts) // blocks, blocks, piece),
        out_shape=[jax.ShapeDtypeStruct((rows, width), jnp.bfloat16)] * 2,
        in_specs=[pl.BlockSpec(memory_space=pltpu.SMEM)]
        + [pl.BlockSpec(memory_space=pltpu.VMEM)] * (2 + len(parts)),
        out_specs=[pl.BlockSpec(memory_space=pltpu.VMEM)] * 2,
        compiler_params=pltpu.CompilerParams(vmem_limit_bytes=8 * MIB),
        cost_estimate=pl.CostEstimate(
            flops=10 * rows * width, bytes_accessed=2 * rows * width * 8, transcendentals=rows
        ),
        name="resid_norm",
    )(me, resid, gain.reshape(1, width), *parts)


def experts_kernel(sources, local_experts, step, load, mark_ref, share_ref, *refs):
    ins = refs[:sources]
    weights = refs[sources : sources + 3]
    outs = refs[sources + 3 : 2 * sources + 3]
    refs[2 * sources + 3][0] = mark_ref[0]
    refs = refs[2 * sources + 4 :]
    copies = [[] for _ in range(local_experts)]
    if load:
        held, refs, sems = refs[:3], refs[3:-1], refs[-1]
        for n in range(local_experts):
            for m in range(3):
                copy = pltpu.make_async_copy(weights[m].at[n], held[m].at[n], sems.at[n, m])
                copy.start()
                copies[n].append(copy)
        weights = held
    gate_ref, up_ref, down_ref = weights
    picked, slot_map, slot_share, hidden_rows, slot_out = refs
    rows = ins[0].shape[0]
    _, width, hidden = gate_ref.shape
    before = (
        lax.broadcasted_iota(jnp.int32, (rows, rows), 0)
        < lax.broadcasted_iota(jnp.int32, (rows, rows), 1)
    ).astype(jnp.bfloat16)
    slot = lax.broadcasted_iota(jnp.int32, (CAP, rows), 0).astype(jnp.float32)
    for s in range(sources):
        both = share_ref[s].astype(jnp.float32)
        if both.shape[1] >= 2 * rows:
            both = both[:, :rows] + both[:, rows : 2 * rows]
        else:
            both = both[: both.shape[0] // 2, :rows] + both[both.shape[0] // 2 :, :rows]
        expert = lax.broadcasted_iota(jnp.int32, both.shape, 0)
        place = lax.broadcasted_iota(jnp.int32, (8, rows), 0)
        share = jnp.zeros((8, rows), jnp.float32)
        for n in range(local_experts):
            mine = jnp.where(expert == mark_ref[0] * local_experts + n, both, 0.0)
            share = jnp.where(place == n, jnp.sum(mine, axis=0, keepdims=True), share)
        rank = dot((share > 0.0).astype(jnp.bfloat16), before)
        rank = jnp.where(share > 0.0, rank, -1.0)
        for n in range(local_experts):
            taken = slot == rank[n : n + 1, :]
            slot_map[s, n * CAP : (n + 1) * CAP, :] = taken.astype(jnp.bfloat16)
            slot_share[n, s * CAP : (s + 1) * CAP, :] = jnp.sum(
                jnp.where(taken, share[n : n + 1, :], 0.0), axis=1, keepdims=True
            )
        rows_picked = dot(slot_map[s], ins[s][...]).astype(jnp.bfloat16)
        for n in range(local_experts):
            picked[n, s * CAP : (s + 1) * CAP, :] = rows_picked[n * CAP : (n + 1) * CAP]
    for n in range(local_experts):
        for copy in copies[n]:
            copy.wait()
        x = picked[n]
        for at in range(0, hidden, step):
            gate_part = dot(x, gate_ref[n, :, at : at + step])
            up_part = dot(x, up_ref[n, :, at : at + step])
            activated = gate_part / (1.0 + jnp.exp(-gate_part)) * up_part * slot_share[n]
            hidden_rows[:, at : at + step] = activated.astype(jnp.bfloat16)
        for at in range(0, width, 2 * step):
            y = dot(hidden_rows[...], down_ref[n, :, at : at + 2 * step]).astype(jnp.bfloat16)
            for s in range(sources):
                slot_out[s, n * CAP : (n + 1) * CAP, at : at + 2 * step] = y[
                    s * CAP : (s + 1) * CAP
                ]
    for s in range(sources):
        outs[s][...] = lax.dot_general(
            slot_map[s], slot_out[s], (((0,), (0,)), ((), ())), preferred_element_type=jnp.float32
        ).astype(jnp.bfloat16)


def experts_call(mark, share, tokens, weights, load, step=256):
    sources = len(tokens)
    rows, width = tokens[0].shape
    local_experts, _, hidden = weights[0].shape
    slots = sources * CAP
    in_vmem = pl.BlockSpec(memory_space=pltpu.VMEM)
    held = [pltpu.VMEM(w.shape, w.dtype) for w in weights] if load else []
    outs = pl.pallas_call(
        functools.partial(experts_kernel, sources, local_experts, step, load),
        out_shape=[jax.ShapeDtypeStruct((rows, width), jnp.bfloat16)] * sources
        + [jax.ShapeDtypeStruct((1,), jnp.int32)]
        + held,
        in_specs=[pl.BlockSpec(memory_space=pltpu.SMEM)]
        + [in_vmem] * (sources + 1)
        + [pl.BlockSpec(memory_space=pl.ANY) if load else in_vmem] * 3,
        out_specs=[in_vmem] * sources
        + [pl.BlockSpec(memory_space=pltpu.SMEM)]
        + [in_vmem] * len(held),
        scratch_shapes=[
            pltpu.VMEM((local_experts, slots, width), jnp.bfloat16),
            pltpu.VMEM((sources, local_experts * CAP, rows), jnp.bfloat16),
            pltpu.VMEM((local_experts, slots, 1), jnp.float32),
            pltpu.VMEM((slots, hidden), jnp.bfloat16),
            pltpu.VMEM((sources, local_experts * CAP, width), jnp.bfloat16),
        ]
        + ([pltpu.SemaphoreType.DMA((local_experts, 3))] if load else []),
        compiler_params=pltpu.CompilerParams(vmem_limit_bytes=(VMEM_EXPERTS_FIRST if load else VMEM_EXPERTS) * MIB),
        cost_estimate=pl.CostEstimate(
            flops=6 * local_experts * slots * width * hidden,
            bytes_accessed=2 * (3 * local_experts * width * hidden + 2 * sources * rows * width),
            transcendentals=local_experts * slots * hidden,
        ),
        name="experts_first" if load else "experts",
    )(mark, share, *tokens, *weights)
    return list(outs[:sources]), outs[sources], list(outs[sources + 1 :]) if load else weights


def over_line(array, pairs):
    return lax.ppermute(array, "exp", [(2 * a + c, 2 * b + c) for a, b in pairs for c in (0, 1)])


def pick_kernel(mark_ref, relayed_ref, middle_ref, out_ref):
    chip = lax.div(mark_ref[0], 2)
    at_end = (chip == 0) | (chip == 3)

    @pl.when(at_end)
    def _():
        out_ref[...] = relayed_ref[...]

    @pl.when(jnp.logical_not(at_end))
    def _():
        out_ref[...] = middle_ref[...]


def take_far(far, mark, chips):
    if chips != 4:
        return lax.optimization_barrier((far, mark))[0]
    in_vmem = pl.BlockSpec(memory_space=pltpu.VMEM)
    return pl.pallas_call(
        pick_kernel,
        out_shape=jax.ShapeDtypeStruct(far[0].shape, far[0].dtype),
        in_specs=[pl.BlockSpec(memory_space=pltpu.SMEM)] + [in_vmem] * 2,
        out_specs=in_vmem,
        compiler_params=pltpu.CompilerParams(vmem_limit_bytes=4 * MIB),
        cost_estimate=pl.CostEstimate(flops=0, bytes_accessed=6 * far[0].size, transcendentals=0),
        name="pick_far",
    )(mark, *far)


def local(
    queries,
    keys,
    values,
    resid,
    out_weight,
    norm_gain,
    expert_gate,
    expert_up,
    expert_down,
    route_ids,
    route_gates,
):
    rows = queries.shape[1]
    ctx_count = lax.axis_size("ctx")
    exp_count = lax.axis_size("exp")
    chips = exp_count // 2
    ctx_me, exp_me = lax.axis_index("ctx"), lax.axis_index("exp")
    local_experts = expert_gate.shape[0]
    heads = QUERY_HEAD_COUNT // ctx_count
    group = QUERY_HEAD_COUNT // KEY_VALUE_HEADS
    kv_heads = max(1, heads // group)

    ctx_mark, exp_mark = (jnp.full((1,), me, jnp.int32) for me in (ctx_me, exp_me))
    piece = out_weight.shape[1]

    *blocks_out, pack = prepare_call(
        ctx_mark,
        queries[0],
        keys[0],
        values[0],
        out_weight,
        route_ids[0],
        route_gates[0],
        ctx_count,
        kv_heads,
        local_experts * exp_count,
    )
    blocks_in = blocks_out[:1] + [swap(blocks_out[j], "ctx", j) for j in range(1, ctx_count)]
    last = chips - 1
    pack_chips = [swap(pack, "exp", 2 * k) for k in range(1, last)]

    att = attention_call(ctx_mark, blocks_in, heads, kv_heads)
    pack_mine, pack_chips[0], att = lax.optimization_barrier((pack, pack_chips[0], att))
    if chips == 4:
        two, pack_mine, att = lax.optimization_barrier((pack_chips[1], pack_mine, att))
        pack_chips[1] = two
        middle = over_line(pack_mine, [(1, 2), (2, 1)])
        pack_far = (over_line(two, [(2, 3), (1, 0)]), middle)
    else:
        pack_far = swap(pack, "exp", 2 * last)

    def project(some):
        mine = projection_call(att, some, ctx_count)
        return [mine[0]] + [swap(mine[j], "ctx", j) for j in range(1, ctx_count)]

    def with_pair(arrays):
        return [both for a in arrays for both in (a, swap(a, "exp", 1))]

    packs = with_pair([pack_mine, pack_chips[0]])
    parts = project(packs)
    packs_middle = with_pair(pack_chips[1:])
    parts_middle = project(packs_middle)
    pack_far, parts, parts_middle[0] = lax.optimization_barrier((pack_far, parts, parts_middle[0]))
    packs_last = with_pair([take_far(pack_far, exp_mark, chips)])
    parts = parts + parts_middle + project(packs_last)
    share = jnp.stack([p[out_weight.shape[0] :] for p in packs + packs_middle + packs_last])
    parts[0], share = lax.optimization_barrier((parts[0], share))
    attn_resid, normed = norm_call(exp_mark, resid[0], norm_gain, parts, ctx_count, piece)

    def experts(which, mark, tokens, weights):
        at = slice(2 * which.start, 2 * which.stop)
        return experts_call(mark, share[at], with_pair(tokens), weights, which.start == 0)

    def pair_sum(both):
        return both[0].astype(jnp.float32) + swap(both[1], "exp", 1).astype(jnp.float32)

    near = [swap(normed, "exp", 2 * k) for k in range(1, last)]
    partial, mark, weights = experts(
        slice(0, 1), exp_mark, [normed], [expert_gate, expert_up, expert_down]
    )
    if chips == 4:
        near[1], normed, mark = lax.optimization_barrier((near[1], normed, mark))
        far = (
            over_line(near[1], [(2, 3), (1, 0)]),
            over_line(normed, [(1, 2), (2, 1)]),
        )
    else:
        far = swap(normed, "exp", 2 * last)
    layer_out = attn_resid.astype(jnp.float32) + pair_sum(partial)
    partial, mark, _ = experts(slice(1, last), mark, near, weights)
    sums = [pair_sum(partial[2 * k :]).astype(jnp.bfloat16) for k in range(last - 1)]
    partial, _, _ = experts(slice(last, chips), mark, [take_far(far, mark, chips)], weights)
    sum_far = pair_sum(partial).astype(jnp.bfloat16)
    if chips == 4:
        def add(a, b):
            return (a.astype(jnp.float32) + b.astype(jnp.float32)).astype(jnp.bfloat16)

        relayed = over_line(sum_far, [(3, 2), (0, 1)])
        early = swap(sums[1], "exp", 2)
        middle = over_line(add(sum_far, early), [(1, 2), (2, 1)])
        both, middle = lax.optimization_barrier((add(sums[1], relayed), middle))
        terms = [swap(sums[0], "exp", 2), middle]
        final = over_line(both, [(2, 0), (1, 3)])
    else:
        terms = [swap(p, "exp", 2 * k) for k, p in enumerate(sums, 1)]
        final = swap(sum_far, "exp", 2 * last)
    for s in terms:
        layer_out = layer_out + s.astype(jnp.float32)
    layer_out = lax.optimization_barrier(layer_out) + final.astype(jnp.float32)
    return (attn_resid[None], layer_out.astype(jnp.bfloat16)[None])


def solution(mesh):
    in_specs = (
        P("exp", "ctx", None),
        P("exp", "ctx", None),
        P("exp", "ctx", None),
        P("exp", "ctx", None),
        P("ctx", "exp"),
        P(),
        P("exp", None, None),
        P("exp", None, None),
        P("exp", None, None),
        P("exp", "ctx", None),
        P("exp", "ctx", None),
    )
    out_specs = (P("exp", "ctx", None), P("exp", "ctx", None))
    return jax.shard_map(local, mesh=mesh, in_specs=in_specs, out_specs=out_specs, check_vma=False)
```
